32 devices in a mesh: groups: 2 (over y), visit: 4 (over z), strip: 2 (over x), band: 2 (over core).
Axes of the slice: x: 2, y: 2, z: 4, core: 2. Of those that a mesh axis runs over, the one named last changes fastest.
Arguments:
- images: bfloat16 [2, 128, 128, 256], P('band', ('groups', 'visit'), 'strip'), parts along dimension 1, may hold values from -8 to 8
- mask_bits: int32 [2, 128, 128, 256], P('band', ('groups', 'visit'), 'strip'), parts along dimension 1, may hold values from 0 to 15
- visit_weight: bfloat16 [2, 128], P('band', ('groups', 'visit')), parts along dimension 1, may hold values from 1 to 4
- intersection: int32 [128, 1], P(('groups', 'visit')), parts along dimension 0, may hold values from 0 to 3, as said below
- patch_owner: int32 [8], P('groups'), parts along dimension 0, may hold values from 0 to 3, each once
Outputs:
- coadd_image: bfloat16 [2, 8, 128, 256], P('band', ('groups', 'visit'), 'strip'), parts along dimension 1
- difference: bfloat16 [2, 128, 128, 256], P('band', ('groups', 'visit'), 'strip'), parts along dimension 1
The draws below stay inside these ranges and needn't reach their ends.
There are 2 independent parts, one for each index of `groups`. The reference program is written for one: setup_inputs(seed, part) draws one part's arguments, and reference() takes and returns one part's arrays. A program takes and returns all parts, laid end to end along the dimension named above; each array names one. Nothing has to cross between parts.
Inputs may be any that keep to these rules, and one draw needn't show every extreme that they name: `intersection`: row j names the patch that piece j intersections. The 16 pieces of one visit index intersect 16 // 8 distinct patches, exactly 8 pieces each; one patch is intersected by 8 pieces of every visit index, and every patch is intersected by some piece. `patch_owner`: A permutation of the patches.
All inputs are finite; a program needn't handle non-finite values.
Results may differ from the reference program's by a relative error of at most 0.0071.
Values may be sent and summed in bfloat16 or wider, within the bound.
No kernel may reach another device: no remote copies, remote signals or barrier semaphores. Data moves between devices by JAX's collectives and lax.ppermute only.
A program may use at most 64 MiB of HBM per device.

```python
import math
import jax
import jax.numpy as jnp
from jax import lax

COLS = 256
PIECES_DEV = 16
CAP = 8
BASES = 6
HALF = 9
PATCHES = 4
PIECES = 64
ROWS = 128
BANDS = 2


basis_rows = (0, 0, 1, 0, 2, 1)


basis_cols = (0, 1, 0, 2, 0, 1)


def tap_rows():
    offsets = jnp.arange(2 * HALF + 1).astype(jnp.float32) - HALF
    gaussian = jnp.exp(-offsets * offsets / 18.0)
    centre = jnp.sum(offsets * offsets * gaussian * gaussian) / jnp.sum(gaussian * gaussian)
    tap_table = jnp.stack([gaussian, offsets * gaussian, (offsets * offsets - centre) * gaussian])
    return tap_table / jnp.sqrt(jnp.sum(tap_table * tap_table, axis=1, keepdims=True))


def intersection_table(key):
    base_key = jax.random.fold_in(key, 7001)
    ranking_key, turn_key, order_key = jax.random.split(base_key, 3)
    ranking = jax.random.permutation(ranking_key, PATCHES).astype(jnp.int32)
    rotate = jax.random.randint(turn_key, (), 0, PATCHES - 1).astype(jnp.int32)
    position = jnp.arange(PIECES).astype(jnp.int32)
    visit_index = position // PIECES_DEV
    local_index = position % PIECES_DEV
    group = local_index // CAP
    rank_index = jnp.where(group == 0, 0, 1 + (rotate + visit_index + group - 1) % (PATCHES - 1))
    ordered = ranking[rank_index]

    def shuffle_block(block_key):
        return jax.random.permutation(block_key, PIECES_DEV).astype(jnp.int32)
    shuffles = jax.vmap(shuffle_block)(jax.random.split(order_key, PATCHES))
    chosen = (jnp.arange(PATCHES).astype(jnp.int32)[:, None] * PIECES_DEV + shuffles).reshape(PIECES)
    return ordered[chosen].astype(jnp.int32)


def draw_intersection(key, part):
    return intersection_table(key)[:, None]


def draw_images(key, part):
    patch_ids = intersection_table(key)
    base_key = jax.random.fold_in(key, 7103)
    sky_key, mixing_key, noise_key, scale_key = jax.random.split(base_key, 4)
    sky_field = jax.random.normal(sky_key, (BANDS, PATCHES, ROWS, COLS), jnp.float32)
    taps = tap_rows()
    padded = jnp.pad(sky_field, ((0, 0), (0, 0), (HALF, HALF), (0, 0)))
    vertical = jnp.zeros((3, BANDS, PATCHES, ROWS, COLS), jnp.float32)
    for offset_index in range(2 * HALF + 1):
        vertical = vertical + taps[:, offset_index, None, None, None, None] * padded[None, :, :, offset_index:offset_index + ROWS]
    widened = jnp.pad(vertical, ((0, 0), (0, 0), (0, 0), (0, 0), (HALF, HALF)))
    plane_list = []
    for basis_index in range(BASES):
        total = jnp.zeros((BANDS, PATCHES, ROWS, COLS), jnp.float32)
        for offset_index in range(2 * HALF + 1):
            total = total + taps[basis_cols[basis_index], offset_index] * widened[basis_rows[basis_index], :, :, :, offset_index:offset_index + COLS]
        plane_list.append(total)
    planes = jnp.stack(plane_list)
    mixing = 0.5 * jax.random.normal(mixing_key, (PIECES, BASES), jnp.float32)

    def one_piece(piece_index):
        patch = patch_ids[piece_index]
        sky_plane = lax.dynamic_index_in_dim(sky_field, patch, 1, keepdims=False)
        convolved = lax.dynamic_index_in_dim(planes, patch, 2, keepdims=False)
        piece_key = jax.random.fold_in(noise_key, piece_index)
        noise = 0.3 * jax.random.normal(piece_key, (BANDS, ROWS, COLS), jnp.float32)
        mixed = jnp.sum(mixing[piece_index][:, None, None, None] * convolved, axis=0)
        return sky_plane + mixed + noise
    pieces_all = lax.map(one_piece, jnp.arange(PIECES).astype(jnp.int32))
    result = jnp.clip(jnp.transpose(pieces_all, (1, 0, 2, 3)), -8.0, 8.0)
    return result.astype(jnp.bfloat16)


def set_ends(entries, key, smallest, high):
    extent = entries.shape
    spot = [jax.random.randint(jax.random.fold_in(key, axis), (), 0, extent[axis]) for axis in range(len(extent))]
    entries = entries.at[tuple(spot)].set(smallest)
    longest = extent.index(max(extent))
    spot[longest] = (spot[longest] + 1) % extent[longest]
    return entries.at[tuple(spot)].set(high)


def block_scale(key, dims, shards, smallest, top_value):
    def one(dim, blocks):
        draws = jax.random.uniform(jax.random.fold_in(jax.random.fold_in(key, 6), dim), (blocks,), jnp.float32, smallest / len(shards), top_value / len(shards))
        return jnp.repeat(jnp.exp(draws), dims[dim] // blocks).reshape((-1,) + (1,) * (len(dims) - dim - 1))

    loudness = one(*shards[0])
    for cut in shards[1:]:
        loudness = loudness * one(*cut)
    return loudness


def setup_inputs(seed: int = 0, part: int = 0) -> dict:
    arg_keys = jax.random.split(jax.random.key(seed), 6)
    part_splits = jax.random.split(jax.random.fold_in(arg_keys[5], part), 6)
    return {
        "images": draw_images(jax.random.fold_in(jax.random.fold_in(arg_keys[5], part), 71), part),
        "mask_bits": set_ends(jax.random.randint(part_splits[1], (BANDS, PIECES, ROWS, COLS), 0, 16), jax.random.fold_in(part_splits[1], 1), 0, 15).astype(jnp.int32),
        "visit_weight": jnp.clip(jnp.exp(math.log(4.0) - 1.3862944 * jax.random.uniform(part_splits[2], (BANDS, PIECES), jnp.float32) ** block_scale(part_splits[2], (BANDS, PIECES), ((0, 2), (1, 4)), -0.2, 0.2)), 1.0, 4.0).astype(jnp.bfloat16),
        "intersection": draw_intersection(jax.random.fold_in(jax.random.fold_in(arg_keys[5], part), 71), part),
        "patch_owner": jax.random.permutation(part_splits[4], PATCHES).astype(jnp.int32),
    }


basis_rows = (0, 0, 1, 0, 2, 1)
basis_cols = (0, 1, 0, 2, 0, 1)

def kernel_taps():
    offsets = jnp.arange(2 * HALF + 1).astype(jnp.float32) - HALF
    gaussian = jnp.exp(-offsets * offsets / 18.0)
    centre = jnp.sum(offsets * offsets * gaussian * gaussian) / jnp.sum(gaussian * gaussian)
    tap_table = jnp.stack([gaussian, offsets * gaussian, (offsets * offsets - centre) * gaussian])
    tap_table = tap_table / jnp.sqrt(lax.optimization_barrier(jnp.sum(tap_table * tap_table, axis=1, keepdims=True)))
    return tap_table.astype(jnp.bfloat16)

def solve_small(matrix, right_side):
    dimension = matrix.shape[-1]
    augmented = jnp.concatenate([matrix, right_side[..., None]], axis=-1)
    for column in range(dimension):
        pivot_row = augmented[..., column, :] / augmented[..., column, column:column + 1]
        augmented = augmented - augmented[..., :, column:column + 1] * pivot_row[..., None, :]
        augmented = augmented.at[..., column, :].set(pivot_row)
    return augmented[..., :, dimension]

def reference(images, mask_bits, visit_weight, intersection, patch_owner):
    usable = (jnp.bitwise_and(mask_bits, 3) != 3).astype(jnp.bfloat16)
    weighted = visit_weight[:, :, None, None] * usable
    patch_ids = intersection[:, 0]
    band_count = images.shape[0]
    zero_planes = jnp.zeros((band_count, PATCHES, ROWS, COLS), jnp.float32)

    def accumulate(carry, piece_index):
        numerator, denominator = carry
        weight_plane = lax.dynamic_index_in_dim(weighted, piece_index, 1, keepdims=False).astype(jnp.float32)
        image_plane = lax.dynamic_index_in_dim(images, piece_index, 1, keepdims=False).astype(jnp.float32)
        target = patch_ids[piece_index]
        numerator = numerator.at[:, target].add(weight_plane * image_plane)
        denominator = denominator.at[:, target].add(weight_plane)
        return ((numerator, denominator), None)
    (numerator, denominator), _ = lax.scan(accumulate, (zero_planes, zero_planes), jnp.arange(PIECES))
    coadd_patch = (numerator / jnp.maximum(denominator, 1.0)).astype(jnp.bfloat16)
    coadd_image = jnp.zeros_like(coadd_patch).at[:, patch_owner].set(coadd_patch)
    taps_float = kernel_taps().astype(jnp.float32)

    def per_piece(piece_index):
        template = jnp.take(coadd_patch, patch_ids[piece_index], axis=1).astype(jnp.float32)
        padded = jnp.pad(template, ((0, 0), (HALF, HALF), (0, 0)))
        smooth = jnp.zeros((3, band_count, ROWS, COLS), jnp.float32)
        for offset_index in range(2 * HALF + 1):
            smooth = smooth + taps_float[:, offset_index, None, None, None] * padded[None, :, offset_index:offset_index + ROWS]
        smooth = smooth.astype(jnp.bfloat16)
        widened = jnp.pad(smooth.astype(jnp.float32), ((0, 0), (0, 0), (0, 0), (HALF, HALF)))
        planes = []
        for basis_index in range(BASES):
            total = jnp.zeros((band_count, ROWS, COLS), jnp.float32)
            for offset_index in range(2 * HALF + 1):
                total = total + taps_float[basis_cols[basis_index], offset_index] * widened[basis_rows[basis_index], :, :, offset_index:offset_index + COLS]
            planes.append(total.astype(jnp.bfloat16))
        basis = jnp.stack(planes).astype(jnp.float32)
        usable_plane = lax.dynamic_index_in_dim(usable, piece_index, 1, keepdims=False).astype(jnp.float32)
        science = lax.dynamic_index_in_dim(images, piece_index, 1, keepdims=False).astype(jnp.float32)
        masked = basis * usable_plane[None]
        normal = jnp.einsum('abyx,cbyx->bac', masked, basis, precision=lax.Precision.HIGHEST)
        right_side = jnp.einsum('abyx,byx->ba', masked, science, precision=lax.Precision.HIGHEST)
        coefficients = solve_small(normal + jnp.eye(BASES, dtype=jnp.float32), right_side)
        fitted = jnp.einsum('ba,abyx->byx', coefficients, basis, precision=lax.Precision.HIGHEST)
        return (science - fitted).astype(jnp.bfloat16)
    difference = jnp.transpose(lax.map(per_piece, jnp.arange(PIECES)), (1, 0, 2, 3))
    return (coadd_image, difference)
```

```python
import functools

import jax
import jax.numpy as jnp
import ml_dtypes
import numpy as np
from jax import lax
from jax.experimental import pallas as pl
from jax.experimental.pallas import tpu as pltpu
from jax.sharding import PartitionSpec as P

BASES = 6
HALF = 9
TILE = 16
basis_rows = (0, 0, 1, 0, 2, 1)
basis_cols = (0, 1, 0, 2, 0, 1)
VMEM_LIMIT = 48 * 1024 * 1024

VMEM = pl.BlockSpec(memory_space=pltpu.VMEM)
SMEM = pl.BlockSpec(memory_space=pltpu.SMEM)


def tap_rows():
    offsets = np.arange(2 * HALF + 1).astype(np.float64) - HALF
    gaussian = np.exp(-offsets * offsets / 18.0)
    squared = gaussian * gaussian
    centre = np.sum(offsets * offsets * squared) / np.sum(squared)
    table = np.stack([gaussian, offsets * gaussian, (offsets * offsets - centre) * gaussian])
    table = table / np.sqrt(np.sum(table * table, axis=1, keepdims=True))
    return table.astype(ml_dtypes.bfloat16)


def across_matrices(cols):
    taps = tap_rows()
    distance = np.arange(cols)[:, None] - np.arange(cols)[None, :] + HALF
    inside = (distance >= 0) & (distance <= 2 * HALF)
    return np.where(inside[None], taps[:, np.clip(distance, 0, 2 * HALF)], 0).astype(ml_dtypes.bfloat16)


def vertical_matrix(rows, sources):
    taps = tap_rows()
    distance = np.asarray(sources)[None, :] - np.arange(rows)[:, None] + HALF
    inside = (distance >= 0) & (distance <= 2 * HALF)
    table = np.where(inside[None], taps[:, np.clip(distance, 0, 2 * HALF)], 0)
    return table.reshape(3 * rows, len(sources)).astype(ml_dtypes.bfloat16)


def unusable(mask):
    return jnp.bitwise_and(mask, 3) == 3


def partial_kernel(slots, cap, ids_ref, weight_ref, image_ref, mask_ref, message_ref, order_ref):
    pieces, rows, cols = image_ref.shape
    ids = [ids_ref[j] for j in range(pieces)]
    for j in range(pieces):
        place = jnp.int32(0)
        for i in range(pieces):
            if i < j:
                place = place + (ids[i] <= ids[j]).astype(jnp.int32)
            elif i > j:
                place = place + (ids[i] < ids[j]).astype(jnp.int32)
        order_ref[place] = j
    for slot in range(slots):
        for first in range(0, rows, TILE):
            numerator = jnp.zeros((TILE, cols), jnp.float32)
            denominator = jnp.zeros((TILE, cols), jnp.float32)
            for k in range(cap):
                j = order_ref[slot * cap + k]
                bad = unusable(mask_ref[j, first : first + TILE, :])
                weight = jnp.where(bad, 0.0, weight_ref[j])
                denominator = denominator + weight
                numerator = numerator + weight * image_ref[j, first : first + TILE, :].astype(jnp.float32)
            at = slot * 2 * rows + first
            message_ref[at : at + TILE, :] = numerator.astype(jnp.bfloat16)
            message_ref[at + rows : at + rows + TILE, :] = denominator.astype(jnp.bfloat16)
    line = lax.broadcasted_iota(jnp.int32, (TILE, cols), 0)
    labels = jnp.zeros((TILE, cols), jnp.float32)
    for slot in range(slots):
        labels = jnp.where(line == slot, ids_ref[order_ref[slot * cap]].astype(jnp.float32), labels)
    message_ref[slots * 2 * rows :, :] = labels.astype(jnp.bfloat16)


def sort_kernel(slots, cap, order_ref, image_ref, mask_ref, usable_ref, masked_ref):
    rows, cols = image_ref.shape[1:]
    for slot in range(slots):
        for k in range(cap):
            j = order_ref[slot * cap + k]
            for g in range(rows // TILE):
                lines = slice(g * TILE, (g + 1) * TILE)
                usable = jnp.where(unusable(mask_ref[j, lines, :]), 0.0, 1.0).astype(jnp.bfloat16)
                at = (slot, slice(k * TILE, (k + 1) * TILE), slice(g * cols, (g + 1) * cols))
                usable_ref[at] = usable
                masked_ref[at] = usable * image_ref[j, lines, :]


def combine_kernel(slots, count, info_ref, owner_ref, *refs):
    own_ref = refs[0]
    sources, (template_ref, edge_ref, coadd_ref), total_ref = refs[1:-4], refs[-4:-1], refs[-1]
    rows, cols = coadd_ref.shape
    base = slots * 2 * rows
    mine = jnp.int32(0)
    for p in range(owner_ref.shape[0]):
        mine = jnp.where(owner_ref[p] == info_ref[0], p, mine)
    mine = mine.astype(jnp.float32)
    own_labels = own_ref[base:, :].astype(jnp.float32)

    def picks(labels, slot):
        label = labels[slot : slot + 1, :]
        hits = [label == own_labels[t : t + 1, :] for t in range(slots)] + [label == mine]
        return [hit.astype(jnp.float32) for hit in hits]

    def finish(target, numerator, denominator, first):
        coadd = (numerator / jnp.maximum(denominator, 1.0)).astype(jnp.bfloat16)
        if target < slots:
            template_ref[target, first : first + TILE, :] = coadd
        else:
            coadd_ref[first : first + TILE, :] = coadd

    if len(sources) == count:
        hits = [
            [picks(ref[base:, :].astype(jnp.float32), slot) for slot in range(slots)]
            for ref in (own_ref,) + tuple(sources[1:])
        ]
        refs_all = (own_ref,) + tuple(sources[1:])
        for first in range(0, rows, TILE):
            sums = [[jnp.zeros((TILE, cols), jnp.float32) for _ in range(2)] for _ in range(slots + 1)]
            for d, ref in enumerate(refs_all):
                for slot in range(slots):
                    for kind in range(2):
                        at = (slot * 2 + kind) * rows + first
                        value = ref[at : at + TILE, :].astype(jnp.float32)
                        for t in range(slots + 1):
                            if d == 0 and t < slots:
                                if t == slot:
                                    sums[t][kind] = sums[t][kind] + value
                            else:
                                sums[t][kind] = sums[t][kind] + hits[d][slot][t] * value
            for t in range(slots + 1):
                finish(t, sums[t][0], sums[t][1], first)
    else:
        stacked = sources[0]
        total_ref[...] = jnp.zeros_like(total_ref)

        def add_source(d, carry):
            labels = stacked[d, base:, :].astype(jnp.float32)
            for slot in range(slots):
                pick = picks(labels, slot)
                for kind in range(2):
                    at = (slot * 2 + kind) * rows
                    value = stacked[d, at : at + rows, :].astype(jnp.float32)
                    for t in range(slots + 1):
                        total_ref[t, kind] += pick[t] * value
            return carry

        lax.fori_loop(0, count, add_source, 0)
        for t in range(slots + 1):
            for first in range(0, rows, TILE):
                finish(t, total_ref[t, 0, first : first + TILE, :], total_ref[t, 1, first : first + TILE, :], first)
    edges = edge_ref.shape[1] // TILE
    if edges == 1:
        first = pl.multiple_of(jnp.where(info_ref[1] == 0, rows - TILE, 0), TILE)
        edge_ref[...] = template_ref[:, pl.ds(first, TILE), :]
    else:
        edge_ref[:, :TILE, :] = template_ref[:, :TILE, :]
        edge_ref[:, TILE:, :] = template_ref[:, rows - TILE :, :]


def normal_kernel(slots, cap, info_ref, template_ref, *refs):
    halo_refs, (vertical_ref, across_ref, usable_ref, masked_ref) = refs[:-8], refs[-8:-4]
    basis_ref, sums_ref, smooth_ref, left_ref = refs[-4:]
    rows, cols = template_ref.shape[1:]
    tiles = rows // TILE
    which = info_ref[1] if vertical_ref.shape[0] > 1 else 0
    vertical = vertical_ref[which]
    for slot in range(slots):
        extended = jnp.concatenate([template_ref[slot]] + [ref[slot] for ref in halo_refs], axis=0)
        smooth = jnp.dot(vertical, extended, preferred_element_type=jnp.float32)
        for k in range(3):
            smooth_ref[k, slot] = smooth[k * rows : (k + 1) * rows].astype(jnp.bfloat16)
    for c in range(3):
        users = [a for a in range(BASES) if basis_cols[a] == c]
        for slot in range(slots):
            stacked = jnp.concatenate([smooth_ref[basis_rows[a], slot] for a in users], axis=0)
            planes = jnp.dot(stacked, across_ref[c], preferred_element_type=jnp.float32).astype(jnp.bfloat16)
            for n, a in enumerate(users):
                for g in range(tiles):
                    at = n * rows + g * TILE
                    basis_ref[slot, a * TILE : (a + 1) * TILE, g * cols : (g + 1) * cols] = planes[at : at + TILE]
    group = cap * TILE
    height = BASES * group + group
    for slot in range(slots):
        for a in range(BASES):
            plane = basis_ref[slot, a * TILE : (a + 1) * TILE, :]
            for k in range(cap):
                at = a * group + k * TILE
                left_ref[at : at + TILE, :] = plane * usable_ref[slot, k * TILE : (k + 1) * TILE, :]
        left_ref[BASES * group :, :] = masked_ref[slot]
        product = lax.dot_general(
            left_ref[...], basis_ref[slot], (((1,), (1,)), ((), ())), preferred_element_type=jnp.float32
        )
        width = product.shape[1]
        line = lax.broadcasted_iota(jnp.int32, (TILE, width), 0)
        lane = lax.broadcasted_iota(jnp.int32, (TILE, width), 1)
        same = line == lane % TILE
        product = jnp.where(same[None], product.reshape(height // TILE, TILE, width), 0.0)
        product = jnp.sum(product, axis=1)
        product = jnp.concatenate([product, jnp.zeros((height // TILE, 128 - width), jnp.float32)], axis=1)
        for step in (1, 2, 4, 8):
            product = product + pltpu.roll(product, 128 - step, 1)
        lanes = lax.broadcasted_iota(jnp.int32, product.shape, 1)
        product = jnp.where(lanes % TILE == 0, product, 0.0)
        packed = product[:cap]
        for a in range(1, BASES + 1):
            packed = packed + pltpu.roll(product[a * cap : (a + 1) * cap], a, 1)
        sums_ref[slot * cap : (slot + 1) * cap, :] = packed


def fit_kernel(slots, cap, order_ref, *refs):
    sums_refs, (basis_ref, image_ref, difference_ref) = refs[:-3], refs[-3:]
    rows, cols = image_ref.shape[1:]
    tiles = rows // TILE
    total = sums_refs[0][...]
    for ref in sums_refs[1:]:
        total = total + ref[...]
    pieces = total.shape[0]
    lanes = lax.broadcasted_iota(jnp.int32, (pieces, 128), 1)
    starts = lanes % TILE == 0
    table = []
    for c in range(BASES + 1):
        line = total if c == 0 else pltpu.roll(total, 128 - c, 1)
        line = jnp.where(starts, line, 0.0)
        if c < BASES:
            line = line + jnp.where(lanes == c * TILE, 1.0, 0.0)
        table.append(line)
    for k in range(BASES):
        at = k * TILE
        pivot = table[k]
        inverse = 1.0 / pivot[:, at : at + 1]
        for c in range(k + 1, BASES + 1):
            ratio = table[c][:, at : at + 1] * inverse
            table[c] = jnp.where(lanes == at, ratio, table[c] - pivot * ratio)
    spread = table[BASES]
    for step in (1, 2, 4, 8):
        spread = spread + pltpu.roll(spread, step, 1)
    line = lax.broadcasted_iota(jnp.int32, (TILE, 128), 0)
    lane = lax.broadcasted_iota(jnp.int32, (TILE, 128), 1)
    same = (line == lane % TILE) & (lane < BASES * TILE)
    for slot in range(slots):
        blocks = [
            jnp.where(same, spread[slot * cap + k : slot * cap + k + 1, :], 0.0) for k in range(cap)
        ]
        exact = jnp.concatenate(blocks, axis=0)[:, : BASES * TILE]
        high = exact.astype(jnp.bfloat16)
        low = (exact - high.astype(jnp.float32)).astype(jnp.bfloat16)
        basis = basis_ref[slot]
        fitted = jnp.dot(high, basis, preferred_element_type=jnp.float32) + jnp.dot(
            low, basis, preferred_element_type=jnp.float32
        )
        for k in range(cap):
            j = order_ref[slot * cap + k]
            for g in range(tiles):
                part = fitted[k * TILE : (k + 1) * TILE, g * cols : (g + 1) * cols]
                image = image_ref[j, g * TILE : (g + 1) * TILE, :].astype(jnp.float32)
                difference_ref[j, g * TILE : (g + 1) * TILE, :] = (image - part).astype(jnp.bfloat16)


def call(kernel, name, outs, in_specs, out_specs, args, scratch=(), flops=0, size=0):
    return pl.pallas_call(
        kernel,
        out_shape=outs,
        in_specs=in_specs,
        out_specs=out_specs,
        scratch_shapes=list(scratch),
        name=name,
        compiler_params=pltpu.CompilerParams(vmem_limit_bytes=VMEM_LIMIT),
        cost_estimate=pl.CostEstimate(flops=flops, bytes_accessed=size, transcendentals=0),
    )(*args)


def body(images, mask_bits, visit_weight, intersection, patch_owner):
    visits = lax.axis_size("visit")
    strips = lax.axis_size("strip")
    _, pieces, rows, cols = images.shape
    slots = visits // 2
    cap = pieces // slots
    tiles = rows // TILE
    shape = jax.ShapeDtypeStruct
    bf16, f32 = jnp.bfloat16, jnp.float32
    image = images[0]
    mask = mask_bits[0]
    ids = intersection[:, 0]
    info = jnp.stack([lax.axis_index("visit"), lax.axis_index("strip")]).astype(jnp.int32)
    label_rows = -(-slots // TILE) * TILE
    message_rows = slots * 2 * rows + label_rows

    message, order = call(
        functools.partial(partial_kernel, slots, cap),
        "partial_sums",
        (shape((message_rows, cols), bf16), shape((pieces,), jnp.int32)),
        [SMEM, SMEM, VMEM, VMEM],
        (VMEM, SMEM),
        (ids, visit_weight[0].astype(f32), image, mask),
        size=2 << 20,
    )
    if visits <= 4:
        received = [
            lax.ppermute(message, "visit", [(i, (i + shift) % visits) for i in range(visits)])
            for shift in range(1, visits)
        ]
        sources = [message] + received
    else:
        sources = [lax.all_gather(message, "visit")]
    usable, masked = call(
        functools.partial(sort_kernel, slots, cap),
        "sorted_usable",
        (shape((slots, cap * TILE, tiles * cols), bf16),) * 2,
        [SMEM, VMEM, VMEM],
        (VMEM, VMEM),
        (order, image, mask),
        size=3 << 20,
    )
    edges = 1 if strips == 2 else 2
    stacked = len(sources) == 1
    template, edge, coadd = call(
        functools.partial(combine_kernel, slots, visits),
        "combine",
        (shape((slots, rows, cols), bf16), shape((slots, edges * TILE, cols), bf16), shape((rows, cols), bf16)),
        [SMEM, SMEM] + [VMEM] * (len(sources) + 1),
        (VMEM,) * 3,
        (info, patch_owner, message, *sources),
        scratch=[pltpu.VMEM((slots + 1, 2, rows, cols) if stacked else (1, 2, TILE, cols), f32)],
        size=1 << 20,
    )
    if strips == 2:
        halos = [lax.ppermute(edge, "strip", [(0, 1), (1, 0)])]
        inside = list(range(rows))
        below = inside + list(range(rows, rows + TILE))
        above = inside + list(range(-TILE, 0))
        vertical = np.stack([vertical_matrix(rows, below), vertical_matrix(rows, above)])
    else:
        halos = [
            lax.ppermute(edge[:, TILE:], "strip", [(i, i + 1) for i in range(strips - 1)]),
            lax.ppermute(edge[:, :TILE], "strip", [(i + 1, i) for i in range(strips - 1)]),
        ]
        around = list(range(rows)) + list(range(-TILE, 0)) + list(range(rows, rows + TILE))
        vertical = vertical_matrix(rows, around)[None]
    basis, sums = call(
        functools.partial(normal_kernel, slots, cap),
        "normal_equations",
        (shape((slots, BASES * TILE, tiles * cols), bf16), shape((pieces, 128), f32)),
        [SMEM] + [VMEM] * (len(halos) + 5),
        (VMEM, VMEM),
        (info, template, *halos, jnp.asarray(vertical), jnp.asarray(across_matrices(cols)), usable, masked),
        scratch=[
            pltpu.VMEM((3, slots, rows, cols), bf16),
            pltpu.VMEM(((BASES + 1) * cap * TILE, tiles * cols), bf16),
        ],
        size=2 << 20,
    )
    if strips == 2:
        totals = [sums, lax.ppermute(sums, "strip", [(0, 1), (1, 0)])]
    else:
        totals = [lax.psum(sums, "strip")]
    difference = call(
        functools.partial(fit_kernel, slots, cap),
        "fit",
        shape((pieces, rows, cols), bf16),
        [SMEM] + [VMEM] * (len(totals) + 2),
        VMEM,
        (order, *totals, basis, image),
        size=2 << 20,
    )
    return (coadd[None, None], difference[None])


def solution(mesh):
    in_specs = (
        P("band", ("groups", "visit"), "strip", None),
        P("band", ("groups", "visit"), "strip", None),
        P("band", ("groups", "visit")),
        P(("groups", "visit"), None),
        P("groups"),
    )
    out_specs = (
        P("band", ("groups", "visit"), "strip", None),
        P("band", ("groups", "visit"), "strip", None),
    )
    return jax.shard_map(body, mesh=mesh, in_specs=in_specs, out_specs=out_specs, check_vma=False)
```

```python
import functools

import jax
import jax.numpy as jnp
import ml_dtypes
import numpy as np
from jax import lax
from jax.experimental import pallas as pl
from jax.experimental.pallas import tpu as pltpu
from jax.sharding import PartitionSpec as P

BASES = 6
HALF = 9
TILE = 16
basis_rows = (0, 0, 1, 0, 2, 1)
basis_cols = (0, 1, 0, 2, 0, 1)
VMEM_LIMIT = 48 * 1024 * 1024
FETCH_LIMIT = 56 * 1024 * 1024

VMEM = pl.BlockSpec(memory_space=pltpu.VMEM)
SMEM = pl.BlockSpec(memory_space=pltpu.SMEM)
HBM = pl.BlockSpec(memory_space=pltpu.HBM)


def tap_rows():
    offsets = np.arange(2 * HALF + 1).astype(np.float64) - HALF
    gaussian = np.exp(-offsets * offsets / 18.0)
    squared = gaussian * gaussian
    centre = np.sum(offsets * offsets * squared) / np.sum(squared)
    table = np.stack([gaussian, offsets * gaussian, (offsets * offsets - centre) * gaussian])
    table = table / np.sqrt(np.sum(table * table, axis=1, keepdims=True))
    return table.astype(ml_dtypes.bfloat16)


def across_matrices(cols):
    taps = tap_rows()
    distance = np.arange(cols)[:, None] - np.arange(cols)[None, :] + HALF
    inside = (distance >= 0) & (distance <= 2 * HALF)
    return np.where(inside[None], taps[:, np.clip(distance, 0, 2 * HALF)], 0).astype(ml_dtypes.bfloat16)


def vertical_matrix(rows, sources):
    taps = tap_rows()
    distance = np.asarray(sources)[None, :] - np.arange(rows)[:, None] + HALF
    inside = (distance >= 0) & (distance <= 2 * HALF)
    table = np.where(inside[None], taps[:, np.clip(distance, 0, 2 * HALF)], 0)
    return table.reshape(3 * rows, len(sources)).astype(ml_dtypes.bfloat16)


def unusable(mask):
    return jnp.bitwise_and(mask, 3) == 3


def piece_order(ids_ref, order_ref):
    pieces = order_ref.shape[0]
    ids = [ids_ref[j] for j in range(pieces)]
    for j in range(pieces):
        place = jnp.int32(0)
        for i in range(pieces):
            if i < j:
                place = place + (ids[i] <= ids[j]).astype(jnp.int32)
            elif i > j:
                place = place + (ids[i] < ids[j]).astype(jnp.int32)
        order_ref[place] = j


def piece_weights(weight_ref, splat_ref):
    weights = weight_ref[...].astype(jnp.float32)
    for j in range(splat_ref.shape[0]):
        splat_ref[j] = weights[0, j]


def windows(half, halves):
    if not halves:
        return 0, 0
    strip = lax.axis_index("strip")
    return pl.multiple_of((1 - strip) * half, TILE), pl.multiple_of(strip * half, TILE)


def put_sums(slots, cap, order_ref, weight_ref, image_of, mask_of, message_ref, base):
    cols = message_ref.shape[1]
    for slot in range(slots):
        numerator = jnp.zeros((TILE, cols), jnp.float32)
        denominator = jnp.zeros((TILE, cols), jnp.float32)
        for k in range(cap):
            j = order_ref[slot * cap + k]
            weight = jnp.where(unusable(mask_of(j)), 0.0, weight_ref[j])
            denominator = denominator + weight
            numerator = numerator + weight * image_of(j).astype(jnp.float32)
        at = base + slot * 2 * TILE
        message_ref[at : at + TILE, :] = numerator.astype(jnp.bfloat16)
        message_ref[at + TILE : at + 2 * TILE, :] = denominator.astype(jnp.bfloat16)


def first_kernel(slots, cap, half, halves, ids_hbm, weight_hbm, image_hbm, mask_hbm, message_hbm, *refs):
    message_ref, order_ref, splat_ref, ids_ref, weight_ref, image_ref, mask_ref, small_sem, sem, out_sem = refs
    cols = image_ref.shape[2]
    tiles = half // TILE
    first = windows(half, halves)[0]
    small = [
        pltpu.make_async_copy(ids_hbm, ids_ref, small_sem.at[0]),
        pltpu.make_async_copy(weight_hbm, weight_ref, small_sem.at[1]),
    ]
    large = []
    for g in range(tiles):
        source = pl.ds(first + g * TILE, TILE)
        here = slice(g * TILE, (g + 1) * TILE)
        large.append(
            (
                pltpu.make_async_copy(mask_hbm.at[:, source, :], mask_ref.at[:, here, :], sem.at[g, 0]),
                pltpu.make_async_copy(image_hbm.at[:, source, :], image_ref.at[:, here, :], sem.at[g, 1]),
            )
        )
    for copy in small:
        copy.start()
    for pair in large:
        for copy in pair:
            copy.start()
    for copy in small:
        copy.wait()
    piece_order(ids_ref, order_ref)
    piece_weights(weight_ref, splat_ref)
    label_rows = message_ref.shape[0] - tiles * slots * 2 * TILE
    line = lax.broadcasted_iota(jnp.int32, (label_rows, cols), 0)
    labels = jnp.zeros((label_rows, cols), jnp.float32)
    for slot in range(slots):
        labels = jnp.where(line == slot, ids_ref[order_ref[slot * cap]].astype(jnp.float32), labels)
    message_ref[:label_rows, :] = labels.astype(jnp.bfloat16)
    done, copies = 0, []
    for g in range(tiles):
        for copy in large[g]:
            copy.wait()
        here = slice(g * TILE, (g + 1) * TILE)
        base = label_rows + g * slots * 2 * TILE
        put_sums(
            slots,
            cap,
            order_ref,
            splat_ref,
            lambda j, here=here: image_ref[j, here, :],
            lambda j, here=here: mask_ref[j, here, :],
            message_ref,
            base,
        )
        ready = pl.ds(done, base + slots * 2 * TILE - done)
        copies.append(pltpu.make_async_copy(message_ref.at[ready, :], message_hbm.at[ready, :], out_sem.at[g]))
        copies[-1].start()
        done = base + slots * 2 * TILE
    for copy in copies:
        copy.wait()


def second_kernel(slots, cap, half, ids_ref, weight_ref, image_ref, mask_ref, message_ref, order_ref, splat_ref):
    first = windows(half, True)[1]
    piece_order(ids_ref, order_ref)
    piece_weights(weight_ref, splat_ref)
    for g in range(half // TILE):
        here = pl.ds(first + g * TILE, TILE)
        put_sums(
            slots,
            cap,
            order_ref,
            splat_ref,
            lambda j, here=here: image_ref[j, here, :],
            lambda j, here=here: mask_ref[j, here, :],
            message_ref,
            g * slots * 2 * TILE,
        )


def sort_kernel(slots, cap, ids_ref, image_ref, mask_ref, usable_ref, masked_ref, order_ref):
    rows, cols = image_ref.shape[1:]
    piece_order(ids_ref, order_ref)
    for slot in range(slots):
        for k in range(cap):
            j = order_ref[slot * cap + k]
            for g in range(rows // TILE):
                lines = slice(g * TILE, (g + 1) * TILE)
                usable = jnp.where(unusable(mask_ref[j, lines, :]), 0.0, 1.0).astype(jnp.bfloat16)
                at = (slot, slice(k * TILE, (k + 1) * TILE), slice(g * cols, (g + 1) * cols))
                usable_ref[at] = usable
                masked_ref[at] = usable * image_ref[j, lines, :]


def owned_patch(owner_ref):
    visit = lax.axis_index("visit")
    mine = jnp.int32(0)
    for p in range(owner_ref.shape[0]):
        mine = jnp.where(owner_ref[p] == visit, p, mine)
    return mine.astype(jnp.float32)


def picks(labels, own_labels, mine, slots, slot):
    label = labels[slot : slot + 1, :]
    hits = [label == own_labels[t : t + 1, :] for t in range(slots)] + [label == mine]
    return [hit.astype(jnp.float32) for hit in hits]


def quotient(numerator, denominator):
    return (numerator / jnp.maximum(denominator, 1.0)).astype(jnp.bfloat16)


def combine(slots, rows, base, mine, labels, sources, put):
    cols = sources[0].shape[1]
    labels = [value.astype(jnp.float32) for value in labels]
    hits = [[picks(label, labels[0], mine, slots, slot) for slot in range(slots)] for label in labels]
    for first in range(0, rows, TILE):
        sums = [[jnp.zeros((TILE, cols), jnp.float32) for _ in range(2)] for _ in range(slots + 1)]
        for d, ref in enumerate(sources):
            for slot in range(slots):
                for kind in range(2):
                    at = base + first * slots * 2 + (slot * 2 + kind) * TILE
                    value = ref[at : at + TILE, :].astype(jnp.float32)
                    for t in range(slots + 1):
                        if d == 0 and t < slots:
                            if t == slot:
                                sums[t][kind] = sums[t][kind] + value
                        else:
                            sums[t][kind] = sums[t][kind] + hits[d][slot][t] * value
        for t in range(slots + 1):
            put(t, first, quotient(*sums[t]))


def border_kernel(slots, count, rows, owner_ref, *refs):
    sources, (template_ref, coadd_ref, edge_ref) = refs[:count], refs[count:]
    base = sources[0].shape[0] - rows * slots * 2
    labels = [ref[:base, :] for ref in sources]

    def put(t, first, value):
        if t < slots:
            template_ref[t, first : first + TILE, :] = value
        else:
            coadd_ref[first : first + TILE, :] = value

    combine(slots, rows, base, owned_patch(owner_ref), labels, sources, put)
    at = pl.multiple_of((1 - lax.axis_index("strip")) * (rows - TILE), TILE)
    edge_ref[...] = template_ref[:, pl.ds(at, TILE), :]


def gathered_kernel(slots, owner_ref, stacked_ref, template_ref, coadd_ref, edge_ref, total_ref):
    rows, cols = coadd_ref.shape
    base = stacked_ref.shape[1] - rows * slots * 2
    mine = owned_patch(owner_ref)
    own_labels = stacked_ref[lax.axis_index("visit"), :base, :].astype(jnp.float32)
    total_ref[...] = jnp.zeros_like(total_ref)

    def add_source(d, carry):
        labels = stacked_ref[d, :base, :].astype(jnp.float32)
        for slot in range(slots):
            pick = picks(labels, own_labels, mine, slots, slot)
            for kind in range(2):
                for first in range(0, rows, TILE):
                    at = base + first * slots * 2 + (slot * 2 + kind) * TILE
                    value = stacked_ref[d, at : at + TILE, :].astype(jnp.float32)
                    for t in range(slots + 1):
                        total_ref[t, kind, first : first + TILE, :] += pick[t] * value
        return carry

    lax.fori_loop(0, stacked_ref.shape[0], add_source, 0)
    for t in range(slots):
        template_ref[t] = quotient(total_ref[t, 0], total_ref[t, 1])
    coadd_ref[...] = quotient(total_ref[slots, 0], total_ref[slots, 1])
    edge_ref[:, :TILE, :] = template_ref[:, :TILE, :]
    edge_ref[:, TILE:, :] = template_ref[:, rows - TILE :, :]


def halves_kernel(slots, cap, count, rows, owner_ref, *refs):
    firsts, seconds, refs = refs[:count], refs[count : 2 * count], refs[2 * count :]
    template_ref, halo_ref, coadd_ref, vertical_ref, across_ref, usable_ref, masked_ref = refs[:7]
    basis_ref, sums_ref, whole_ref, second_ref, smooth_ref, left_ref = refs[7:]
    labels = [ref[: ref.shape[0] - rows * slots * 2, :] for ref in firsts]
    early, late = windows(rows, True)
    whole_ref[pl.ds(early, rows), :] = coadd_ref[...]

    def put(t, first, value):
        if t < slots:
            second_ref[t, first : first + TILE, :] = value
        else:
            whole_ref[pl.ds(late + first, TILE), :] = value

    combine(slots, rows, 0, owned_patch(owner_ref), labels, seconds, put)
    normal_equations(
        slots,
        cap,
        [template_ref, second_ref, halo_ref],
        vertical_ref[lax.axis_index("strip")],
        across_ref,
        usable_ref,
        masked_ref,
        basis_ref,
        sums_ref,
        smooth_ref,
        left_ref,
    )


def normal_kernel(slots, cap, template_ref, below_ref, above_ref, vertical_ref, *refs):
    normal_equations(slots, cap, [template_ref, below_ref, above_ref], vertical_ref[0], *refs)


def normal_equations(
    slots, cap, parts, vertical, across_ref, usable_ref, masked_ref, basis_ref, sums_ref, smooth_ref, left_ref
):
    rows, cols = smooth_ref.shape[2:]
    tiles = rows // TILE
    for slot in range(slots):
        extended = jnp.concatenate([ref[slot] for ref in parts], axis=0)
        smooth = jnp.dot(vertical, extended, preferred_element_type=jnp.float32)
        for k in range(3):
            smooth_ref[k, slot] = smooth[k * rows : (k + 1) * rows].astype(jnp.bfloat16)
    for c in range(3):
        users = [a for a in range(BASES) if basis_cols[a] == c]
        for slot in range(slots):
            stacked = jnp.concatenate([smooth_ref[basis_rows[a], slot] for a in users], axis=0)
            planes = jnp.dot(stacked, across_ref[c], preferred_element_type=jnp.float32).astype(jnp.bfloat16)
            for n, a in enumerate(users):
                for g in range(tiles):
                    at = n * rows + g * TILE
                    basis_ref[slot, a * TILE : (a + 1) * TILE, g * cols : (g + 1) * cols] = planes[at : at + TILE]
    group = cap * TILE
    height = BASES * group + group
    for slot in range(slots):
        for a in range(BASES):
            plane = basis_ref[slot, a * TILE : (a + 1) * TILE, :]
            for k in range(cap):
                at = a * group + k * TILE
                left_ref[at : at + TILE, :] = plane * usable_ref[slot, k * TILE : (k + 1) * TILE, :]
        left_ref[BASES * group :, :] = masked_ref[slot]
        product = lax.dot_general(
            left_ref[...], basis_ref[slot], (((1,), (1,)), ((), ())), preferred_element_type=jnp.float32
        )
        width = product.shape[1]
        line = lax.broadcasted_iota(jnp.int32, (TILE, width), 0)
        lane = lax.broadcasted_iota(jnp.int32, (TILE, width), 1)
        same = line == lane % TILE
        product = jnp.where(same[None], product.reshape(height // TILE, TILE, width), 0.0)
        product = jnp.sum(product, axis=1)
        product = jnp.concatenate([product, jnp.zeros((height // TILE, 128 - width), jnp.float32)], axis=1)
        for step in (1, 2, 4, 8):
            product = product + pltpu.roll(product, 128 - step, 1)
        lanes = lax.broadcasted_iota(jnp.int32, product.shape, 1)
        product = jnp.where(lanes % TILE == 0, product, 0.0)
        packed = product[:cap]
        for a in range(1, BASES + 1):
            packed = packed + pltpu.roll(product[a * cap : (a + 1) * cap], a, 1)
        sums_ref[slot * cap : (slot + 1) * cap, :] = packed


def fit_kernel(slots, cap, order_ref, *refs):
    sums_refs, (basis_ref, image_ref, difference_hbm, difference_ref, sem) = refs[:-5], refs[-5:]
    rows, cols = image_ref.shape[1:]
    tiles = rows // TILE
    total = sums_refs[0][...]
    for ref in sums_refs[1:]:
        total = total + ref[...]
    pieces = total.shape[0]
    lanes = lax.broadcasted_iota(jnp.int32, (pieces, 128), 1)
    starts = lanes % TILE == 0
    table = []
    for c in range(BASES + 1):
        line = total if c == 0 else pltpu.roll(total, 128 - c, 1)
        line = jnp.where(starts, line, 0.0)
        if c < BASES:
            line = line + jnp.where(lanes == c * TILE, 1.0, 0.0)
        table.append(line)
    for k in range(BASES):
        at = k * TILE
        pivot = table[k]
        inverse = 1.0 / pivot[:, at : at + 1]
        for c in range(k + 1, BASES + 1):
            ratio = table[c][:, at : at + 1] * inverse
            table[c] = jnp.where(lanes == at, ratio, table[c] - pivot * ratio)
    spread = table[BASES]
    for step in (1, 2, 4, 8):
        spread = spread + pltpu.roll(spread, step, 1)
    line = lax.broadcasted_iota(jnp.int32, (TILE, 128), 0)
    lane = lax.broadcasted_iota(jnp.int32, (TILE, 128), 1)
    same = (line == lane % TILE) & (lane < BASES * TILE)
    copies = []
    for slot in range(slots):
        blocks = [
            jnp.where(same, spread[slot * cap + k : slot * cap + k + 1, :], 0.0) for k in range(cap)
        ]
        exact = jnp.concatenate(blocks, axis=0)[:, : BASES * TILE]
        high = exact.astype(jnp.bfloat16)
        low = (exact - high.astype(jnp.float32)).astype(jnp.bfloat16)
        basis = basis_ref[slot]
        fitted = jnp.dot(high, basis, preferred_element_type=jnp.float32) + jnp.dot(
            low, basis, preferred_element_type=jnp.float32
        )
        for k in range(cap):
            j = order_ref[slot * cap + k]
            place = slot * cap + k
            for g in range(tiles):
                part = fitted[k * TILE : (k + 1) * TILE, g * cols : (g + 1) * cols]
                image = image_ref[j, g * TILE : (g + 1) * TILE, :].astype(jnp.float32)
                difference_ref[place, g * TILE : (g + 1) * TILE, :] = (image - part).astype(jnp.bfloat16)
            copy = pltpu.make_async_copy(difference_ref.at[place], difference_hbm.at[j], sem.at[place])
            copy.start()
            copies.append(copy)
    for copy in copies:
        copy.wait()


def call(kernel, name, outs, in_specs, out_specs, args, scratch=(), flops=0, size=0, limit=VMEM_LIMIT):
    return pl.pallas_call(
        kernel,
        out_shape=outs,
        in_specs=in_specs,
        out_specs=out_specs,
        scratch_shapes=list(scratch),
        name=name,
        compiler_params=pltpu.CompilerParams(vmem_limit_bytes=limit),
        cost_estimate=pl.CostEstimate(flops=flops, bytes_accessed=size, transcendentals=0),
    )(*args)


def body(images, mask_bits, visit_weight, intersection, patch_owner):
    visits = lax.axis_size("visit")
    strips = lax.axis_size("strip")
    _, pieces, rows, cols = images.shape
    slots = visits // 2
    cap = pieces // slots
    tiles = rows // TILE
    shape = jax.ShapeDtypeStruct
    bf16, f32 = jnp.bfloat16, jnp.float32
    image = images[0]
    mask = mask_bits[0]
    halves = strips == 2 and visits <= 4
    half = rows // 2 if halves else rows
    ids = intersection[:, 0]
    label_rows = -(-slots // TILE) * TILE
    message_shape = (label_rows + slots * 2 * half, cols)

    message = call(
        functools.partial(first_kernel, slots, cap, half, halves),
        "first_sums",
        shape(message_shape, bf16),
        [HBM] * 4,
        HBM,
        (ids, visit_weight, image, mask),
        scratch=[
            pltpu.VMEM(message_shape, bf16),
            pltpu.SMEM((pieces,), jnp.int32),
            pltpu.SMEM((pieces,), f32),
            pltpu.SMEM((pieces,), jnp.int32),
            pltpu.VMEM((1, pieces), bf16),
            pltpu.VMEM((pieces, half, cols), bf16),
            pltpu.VMEM((pieces, half, cols), jnp.int32),
            pltpu.SemaphoreType.DMA((2,)),
            pltpu.SemaphoreType.DMA((half // TILE, 2)),
            pltpu.SemaphoreType.DMA((half // TILE,)),
        ],
        size=2 << 20,
        limit=FETCH_LIMIT,
    )

    def everyone(value):
        others = [
            lax.ppermute(value, "visit", [(i, (i + shift) % visits) for i in range(visits)])
            for shift in range(1, visits)
        ]
        return [value] + others

    sorted_shape = shape((slots, cap * TILE, tiles * cols), bf16)
    if halves:
        firsts = everyone(message)
        second = call(
            functools.partial(second_kernel, slots, cap, half),
            "second_sums",
            shape((slots * 2 * half, cols), bf16),
            [SMEM] + [VMEM] * 3,
            VMEM,
            (ids, visit_weight, image, mask),
            scratch=[pltpu.SMEM((pieces,), jnp.int32), pltpu.SMEM((pieces,), f32)],
            size=1 << 20,
        )
        seconds = everyone(second)
    usable, masked, order = call(
        functools.partial(sort_kernel, slots, cap),
        "sorted_usable",
        (sorted_shape, sorted_shape, shape((pieces,), jnp.int32)),
        [SMEM, VMEM, VMEM],
        (VMEM, VMEM, SMEM),
        (ids, image, mask),
        size=3 << 20,
    )
    normal_outs = (shape((slots, BASES * TILE, tiles * cols), bf16), shape((pieces, 128), f32))
    normal_scratch = [
        pltpu.VMEM((3, slots, rows, cols), bf16),
        pltpu.VMEM(((BASES + 1) * cap * TILE, tiles * cols), bf16),
    ]
    across = jnp.asarray(across_matrices(cols))
    if halves:
        template, coadd, edge = call(
            functools.partial(border_kernel, slots, visits, half),
            "border",
            (shape((slots, half, cols), bf16), shape((half, cols), bf16), shape((slots, TILE, cols), bf16)),
            [SMEM] + [VMEM] * visits,
            (VMEM,) * 3,
            (patch_owner, *firsts),
            size=1 << 20,
        )
        halo = lax.ppermute(edge, "strip", [(0, 1), (1, 0)])
        low, high = list(range(half)), list(range(half, rows))
        vertical = np.stack(
            [
                vertical_matrix(rows, high + low + list(range(rows, rows + TILE))),
                vertical_matrix(rows, low + high + list(range(-TILE, 0))),
            ]
        )
        basis, sums, coadd = call(
            functools.partial(halves_kernel, slots, cap, visits, half),
            "normal_equations",
            (*normal_outs, shape((rows, cols), bf16)),
            [SMEM] + [VMEM] * (2 * visits + 7),
            (VMEM,) * 3,
            (
                patch_owner,
                *firsts,
                *seconds,
                template,
                halo,
                coadd,
                jnp.asarray(vertical),
                across,
                usable,
                masked,
            ),
            scratch=[pltpu.VMEM((slots, half, cols), bf16)] + normal_scratch,
            size=2 << 20,
        )
        totals = [sums, lax.ppermute(sums, "strip", [(0, 1), (1, 0)])]
    else:
        template, coadd, edge = call(
            functools.partial(gathered_kernel, slots),
            "combine",
            (shape((slots, rows, cols), bf16), shape((rows, cols), bf16), shape((slots, 2 * TILE, cols), bf16)),
            [SMEM, VMEM],
            (VMEM,) * 3,
            (patch_owner, lax.all_gather(message, "visit")),
            scratch=[pltpu.VMEM((slots + 1, 2, rows, cols), f32)],
            size=1 << 20,
        )
        below = lax.ppermute(edge[:, TILE:], "strip", [(i, i + 1) for i in range(strips - 1)])
        above = lax.ppermute(edge[:, :TILE], "strip", [(i + 1, i) for i in range(strips - 1)])
        around = list(range(rows)) + list(range(-TILE, 0)) + list(range(rows, rows + TILE))
        basis, sums = call(
            functools.partial(normal_kernel, slots, cap),
            "normal_equations",
            normal_outs,
            [VMEM] * 7,
            (VMEM, VMEM),
            (template, below, above, jnp.asarray(vertical_matrix(rows, around)[None]), across, usable, masked),
            scratch=normal_scratch,
            size=2 << 20,
        )
        totals = [lax.psum(sums, "strip")]
    difference = call(
        functools.partial(fit_kernel, slots, cap),
        "fit",
        shape((pieces, rows, cols), bf16),
        [SMEM] + [VMEM] * (len(totals) + 2),
        HBM,
        (order, *totals, basis, image),
        scratch=[pltpu.VMEM((pieces, rows, cols), bf16), pltpu.SemaphoreType.DMA((pieces,))],
        size=2 << 20,
    )
    return (coadd[None, None], difference[None])


def solution(mesh):
    in_specs = (
        P("band", ("groups", "visit"), "strip", None),
        P("band", ("groups", "visit"), "strip", None),
        P("band", ("groups", "visit")),
        P(("groups", "visit"), None),
        P("groups"),
    )
    out_specs = (
        P("band", ("groups", "visit"), "strip", None),
        P("band", ("groups", "visit"), "strip", None),
    )
    return jax.shard_map(body, mesh=mesh, in_specs=in_specs, out_specs=out_specs, check_vma=False)
```

```python
import functools

import jax
import jax.numpy as jnp
import ml_dtypes
import numpy as np
from jax import lax
from jax.experimental import pallas as pl
from jax.experimental.pallas import tpu as pltpu
from jax.sharding import PartitionSpec as P

BASES = 6
HALF = 9
TILE = 16
LANES = 128
basis_rows = (0, 0, 1, 0, 2, 1)
basis_cols = (0, 1, 0, 2, 0, 1)
VMEM_LIMIT = 48 * 1024 * 1024
FETCH_LIMIT = 56 * 1024 * 1024

VMEM = pl.BlockSpec(memory_space=pltpu.VMEM)
SMEM = pl.BlockSpec(memory_space=pltpu.SMEM)
HBM = pl.BlockSpec(memory_space=pltpu.HBM)
ANY = pl.BlockSpec(memory_space=pl.ANY)


def tap_rows():
    offsets = np.arange(2 * HALF + 1).astype(np.float64) - HALF
    gaussian = np.exp(-offsets * offsets / 18.0)
    squared = gaussian * gaussian
    centre = np.sum(offsets * offsets * squared) / np.sum(squared)
    table = np.stack([gaussian, offsets * gaussian, (offsets * offsets - centre) * gaussian])
    table = table / np.sqrt(np.sum(table * table, axis=1, keepdims=True))
    return table.astype(ml_dtypes.bfloat16)


def across_matrices(cols):
    taps = tap_rows()
    distance = np.arange(cols)[:, None] - np.arange(cols)[None, :] + HALF
    inside = (distance >= 0) & (distance <= 2 * HALF)
    return np.where(inside[None], taps[:, np.clip(distance, 0, 2 * HALF)], 0).astype(ml_dtypes.bfloat16)


def vertical_matrix(rows, sources):
    taps = tap_rows()
    distance = np.asarray(sources)[None, :] - np.arange(rows)[:, None] + HALF
    inside = (distance >= 0) & (distance <= 2 * HALF)
    table = np.where(inside[None], taps[:, np.clip(distance, 0, 2 * HALF)], 0)
    return table.reshape(3 * rows, len(sources)).astype(ml_dtypes.bfloat16)


def unusable(mask):
    return jnp.bitwise_and(mask, 3) == 3


def piece_order(ids_ref, order_ref):
    pieces = order_ref.shape[0]
    ids = [ids_ref[j] for j in range(pieces)]
    for j in range(pieces):
        place = jnp.int32(0)
        for i in range(pieces):
            if i < j:
                place = place + (ids[i] <= ids[j]).astype(jnp.int32)
            elif i > j:
                place = place + (ids[i] < ids[j]).astype(jnp.int32)
        order_ref[place] = j


def piece_weights(weight_ref, splat_ref):
    weights = weight_ref[...].astype(jnp.float32)
    for j in range(splat_ref.shape[0]):
        splat_ref[j] = weights[0, j]


def windows(half, halves):
    if not halves:
        return 0, 0
    strip = lax.axis_index("strip")
    return pl.multiple_of((1 - strip) * half, TILE), pl.multiple_of(strip * half, TILE)


def put_sums(slots, cap, order_ref, weight_ref, image_of, mask_of, message_ref, base):
    cols = image_of(0).shape[1]
    parts = cols // LANES
    for slot in range(slots):
        numerator = jnp.zeros((TILE, cols), jnp.float32)
        denominator = jnp.zeros((TILE, cols), jnp.float32)
        for k in range(cap):
            j = order_ref[slot * cap + k]
            weight = jnp.where(unusable(mask_of(j)), 0.0, weight_ref[j])
            denominator = denominator + weight
            numerator = numerator + weight * image_of(j).astype(jnp.float32)
        for kind, value in enumerate((numerator.astype(jnp.bfloat16), denominator.astype(jnp.bfloat16))):
            for part in range(parts):
                at = base + ((slot * 2 + kind) * parts + part) * TILE
                message_ref[at : at + TILE, :] = value[:, part * LANES : (part + 1) * LANES]


def first_kernel(slots, cap, half, halves, ids_hbm, weight_hbm, image_hbm, mask_hbm, message_hbm, *refs):
    message_ref, order_ref, splat_ref, ids_ref, weight_ref, image_ref, mask_ref, small_sem, sem, out_sem = refs
    tiles = half // TILE
    step = slots * 2 * TILE * (image_ref.shape[2] // LANES)
    first = windows(half, halves)[0]
    small = [
        pltpu.make_async_copy(ids_hbm, ids_ref, small_sem.at[0]),
        pltpu.make_async_copy(weight_hbm, weight_ref, small_sem.at[1]),
    ]
    large = []
    for g in range(tiles):
        source = pl.ds(first + g * TILE, TILE)
        here = slice(g * TILE, (g + 1) * TILE)
        large.append(
            (
                pltpu.make_async_copy(mask_hbm.at[:, source, :], mask_ref.at[:, here, :], sem.at[g, 0]),
                pltpu.make_async_copy(image_hbm.at[:, source, :], image_ref.at[:, here, :], sem.at[g, 1]),
            )
        )
    for copy in small:
        copy.start()
    for pair in large:
        for copy in pair:
            copy.start()
    for copy in small:
        copy.wait()
    piece_order(ids_ref, order_ref)
    piece_weights(weight_ref, splat_ref)
    label_rows = message_ref.shape[0] - tiles * step
    line = lax.broadcasted_iota(jnp.int32, (label_rows, LANES), 0)
    labels = jnp.zeros((label_rows, LANES), jnp.float32)
    for slot in range(slots):
        labels = jnp.where(line == slot, ids_ref[order_ref[slot * cap]].astype(jnp.float32), labels)
    message_ref[:label_rows, :] = labels.astype(jnp.bfloat16)
    done, copies = 0, []
    for g in range(tiles):
        for copy in large[g]:
            copy.wait()
        here = slice(g * TILE, (g + 1) * TILE)
        base = label_rows + g * step
        put_sums(
            slots,
            cap,
            order_ref,
            splat_ref,
            lambda j, here=here: image_ref[j, here, :],
            lambda j, here=here: mask_ref[j, here, :],
            message_ref,
            base,
        )
        ready = pl.ds(done, base + step - done)
        copies.append(pltpu.make_async_copy(message_ref.at[ready, :], message_hbm.at[ready, :], out_sem.at[g]))
        copies[-1].start()
        done = base + step
    for copy in copies:
        copy.wait()


def second_kernel(slots, cap, half, ids_ref, weight_ref, image_ref, mask_ref, *refs):
    message_ref, usable_ref, masked_ref, order_ref, splat_ref = refs
    first = windows(half, True)[1]
    step = slots * 2 * TILE * (image_ref.shape[2] // LANES)
    piece_order(ids_ref, order_ref)
    piece_weights(weight_ref, splat_ref)
    for g in range(half // TILE):
        here = pl.ds(first + g * TILE, TILE)
        put_sums(
            slots,
            cap,
            order_ref,
            splat_ref,
            lambda j, here=here: image_ref[j, here, :],
            lambda j, here=here: mask_ref[j, here, :],
            message_ref,
            g * step,
        )
    put_sorted(slots, cap, order_ref, image_ref, mask_ref, usable_ref, masked_ref)


def sort_kernel(slots, cap, ids_ref, image_ref, mask_ref, usable_ref, masked_ref, order_ref):
    piece_order(ids_ref, order_ref)
    put_sorted(slots, cap, order_ref, image_ref, mask_ref, usable_ref, masked_ref)


def put_sorted(slots, cap, order_ref, image_ref, mask_ref, usable_ref, masked_ref):
    rows, cols = image_ref.shape[1:]
    for slot in range(slots):
        for k in range(cap):
            j = order_ref[slot * cap + k]
            for g in range(rows // TILE):
                lines = slice(g * TILE, (g + 1) * TILE)
                usable = jnp.where(unusable(mask_ref[j, lines, :]), 0.0, 1.0).astype(jnp.bfloat16)
                at = (slot, slice(k * TILE, (k + 1) * TILE), slice(g * cols, (g + 1) * cols))
                usable_ref[at] = usable
                masked_ref[at] = usable * image_ref[j, lines, :]


def owned_patch(owner_ref):
    visit = lax.axis_index("visit")
    mine = jnp.int32(0)
    for p in range(owner_ref.shape[0]):
        mine = jnp.where(owner_ref[p] == visit, p, mine)
    return mine.astype(jnp.float32)


def picks(labels, own_labels, mine, slots, slot):
    label = labels[slot : slot + 1, :]
    hits = [label == own_labels[t : t + 1, :] for t in range(slots)] + [label == mine]
    return [hit.astype(jnp.float32) for hit in hits]


def quotient(numerator, denominator):
    return (numerator / jnp.maximum(denominator, 1.0)).astype(jnp.bfloat16)


def combine(slots, rows, cols, base, mine, labels, sources, put):
    parts = cols // LANES
    labels = [value.astype(jnp.float32) for value in labels]
    hits = [[picks(label, labels[0], mine, slots, slot) for slot in range(slots)] for label in labels]
    for first in range(0, rows, TILE):
        for part in range(parts):
            sums = [[jnp.zeros((TILE, LANES), jnp.float32) for _ in range(2)] for _ in range(slots + 1)]
            for d, ref in enumerate(sources):
                for slot in range(slots):
                    for kind in range(2):
                        at = base + (first * slots * 2 + (slot * 2 + kind) * TILE) * parts + part * TILE
                        value = ref[at : at + TILE, :].astype(jnp.float32)
                        for t in range(slots + 1):
                            if d == 0 and t < slots:
                                if t == slot:
                                    sums[t][kind] = sums[t][kind] + value
                            else:
                                sums[t][kind] = sums[t][kind] + hits[d][slot][t] * value
            lanes = slice(part * LANES, (part + 1) * LANES)
            for t in range(slots + 1):
                put(t, first, lanes, quotient(*sums[t]))


def border_kernel(slots, count, rows, owner_ref, *refs):
    sources, (template_ref, coadd_ref, edge_ref, mine_ref) = refs[:count], refs[count:]
    cols = coadd_ref.shape[1]
    base = sources[0].shape[0] - rows * slots * 2 * (cols // LANES)
    labels = [ref[:base, :] for ref in sources]

    def put(t, first, lanes, value):
        if t < slots:
            template_ref[t, first : first + TILE, lanes] = value
        else:
            coadd_ref[first : first + TILE, lanes] = value

    mine_ref[...] = jnp.broadcast_to(owned_patch(owner_ref), mine_ref.shape)
    combine(slots, rows, cols, base, mine_ref[:1, :], labels, sources, put)
    at = pl.multiple_of((1 - lax.axis_index("strip")) * (rows - TILE), TILE)
    edge_ref[...] = template_ref[:, pl.ds(at, TILE), :]


def gathered_kernel(slots, owner_ref, stacked_ref, template_ref, coadd_ref, edge_ref, total_ref):
    rows, cols = coadd_ref.shape
    parts = cols // LANES
    base = stacked_ref.shape[1] - rows * slots * 2 * parts
    mine = owned_patch(owner_ref)
    own_labels = stacked_ref[lax.axis_index("visit"), :base, :].astype(jnp.float32)
    total_ref[...] = jnp.zeros_like(total_ref)

    def add_source(d, carry):
        labels = stacked_ref[d, :base, :].astype(jnp.float32)
        for slot in range(slots):
            pick = picks(labels, own_labels, mine, slots, slot)
            for kind in range(2):
                for first in range(0, rows, TILE):
                    for part in range(parts):
                        at = base + (first * slots * 2 + (slot * 2 + kind) * TILE) * parts + part * TILE
                        value = stacked_ref[d, at : at + TILE, :].astype(jnp.float32)
                        lanes = slice(part * LANES, (part + 1) * LANES)
                        for t in range(slots + 1):
                            total_ref[t, kind, first : first + TILE, lanes] += pick[t] * value
        return carry

    lax.fori_loop(0, stacked_ref.shape[0], add_source, 0)
    for t in range(slots):
        template_ref[t] = quotient(total_ref[t, 0], total_ref[t, 1])
    coadd_ref[...] = quotient(total_ref[slots, 0], total_ref[slots, 1])
    edge_ref[:, :TILE, :] = template_ref[:, :TILE, :]
    edge_ref[:, TILE:, :] = template_ref[:, rows - TILE :, :]


def halves_kernel(slots, cap, count, rows, mine_ref, *refs):
    firsts, seconds, refs = refs[:count], refs[count : 2 * count], refs[2 * count :]
    template_ref, halo_ref, coadd_ref, vertical_ref, across_ref, usable_ref, masked_ref = refs[:7]
    basis_ref, sums_ref, whole_ref, second_ref, smooth_ref, left_ref = refs[7:]
    cols = whole_ref.shape[1]
    labels = [ref[: ref.shape[0] - rows * slots * 2 * (cols // LANES), :] for ref in firsts]
    early, late = windows(rows, True)
    whole_ref[pl.ds(early, rows), :] = coadd_ref[...]

    def put(t, first, lanes, value):
        if t < slots:
            second_ref[t, first : first + TILE, lanes] = value
        else:
            whole_ref[pl.ds(late + first, TILE), lanes] = value

    combine(slots, rows, cols, 0, mine_ref[:1, :], labels, seconds, put)
    normal_equations(
        slots,
        cap,
        [template_ref, second_ref, halo_ref],
        vertical_ref[lax.axis_index("strip")],
        across_ref,
        usable_ref,
        masked_ref,
        basis_ref,
        sums_ref,
        smooth_ref,
        left_ref,
    )


def normal_kernel(slots, cap, template_ref, below_ref, above_ref, vertical_ref, *refs):
    normal_equations(slots, cap, [template_ref, below_ref, above_ref], vertical_ref[0], *refs)


def normal_equations(
    slots, cap, parts, vertical, across_ref, usable_ref, masked_ref, basis_ref, sums_ref, smooth_ref, left_ref
):
    rows, cols = smooth_ref.shape[2:]
    tiles = rows // TILE
    for slot in range(slots):
        extended = jnp.concatenate([ref[slot] for ref in parts], axis=0)
        smooth = jnp.dot(vertical, extended, preferred_element_type=jnp.float32)
        for k in range(3):
            smooth_ref[k, slot] = smooth[k * rows : (k + 1) * rows].astype(jnp.bfloat16)
    for c in range(3):
        users = [a for a in range(BASES) if basis_cols[a] == c]
        for slot in range(slots):
            stacked = jnp.concatenate([smooth_ref[basis_rows[a], slot] for a in users], axis=0)
            planes = jnp.dot(stacked, across_ref[c], preferred_element_type=jnp.float32).astype(jnp.bfloat16)
            for n, a in enumerate(users):
                for g in range(tiles):
                    at = n * rows + g * TILE
                    basis_ref[slot, a * TILE : (a + 1) * TILE, g * cols : (g + 1) * cols] = planes[at : at + TILE]
    group = cap * TILE
    height = BASES * group + group
    for slot in range(slots):
        for a in range(BASES):
            plane = basis_ref[slot, a * TILE : (a + 1) * TILE, :]
            for k in range(cap):
                at = a * group + k * TILE
                left_ref[at : at + TILE, :] = plane * usable_ref[slot, k * TILE : (k + 1) * TILE, :]
        left_ref[BASES * group :, :] = masked_ref[slot]
        product = lax.dot_general(
            left_ref[...], basis_ref[slot], (((1,), (1,)), ((), ())), preferred_element_type=jnp.float32
        )
        width = product.shape[1]
        line = lax.broadcasted_iota(jnp.int32, (TILE, width), 0)
        lane = lax.broadcasted_iota(jnp.int32, (TILE, width), 1)
        same = line == lane % TILE
        product = jnp.where(same[None], product.reshape(height // TILE, TILE, width), 0.0)
        product = jnp.sum(product, axis=1)
        product = jnp.concatenate([product, jnp.zeros((height // TILE, 128 - width), jnp.float32)], axis=1)
        for step in (1, 2, 4, 8):
            product = product + pltpu.roll(product, 128 - step, 1)
        lanes = lax.broadcasted_iota(jnp.int32, product.shape, 1)
        product = jnp.where(lanes % TILE == 0, product, 0.0)
        packed = product[:cap]
        for a in range(1, BASES + 1):
            packed = packed + pltpu.roll(product[a * cap : (a + 1) * cap], a, 1)
        sums_ref[slot * cap : (slot + 1) * cap, :] = packed


def fit_kernel(slots, cap, order_any, *refs):
    sums_refs, refs = refs[:-7], refs[-7:]
    basis_ref, image_ref, difference_hbm, difference_ref, order_ref, order_sem, sem = refs
    order_copy = pltpu.make_async_copy(order_any, order_ref, order_sem.at[0])
    order_copy.start()
    rows, cols = image_ref.shape[1:]
    tiles = rows // TILE
    total = sums_refs[0][...]
    for ref in sums_refs[1:]:
        total = total + ref[...]
    pieces = total.shape[0]
    lanes = lax.broadcasted_iota(jnp.int32, (pieces, 128), 1)
    starts = lanes % TILE == 0
    table = []
    for c in range(BASES + 1):
        line = total if c == 0 else pltpu.roll(total, 128 - c, 1)
        line = jnp.where(starts, line, 0.0)
        if c < BASES:
            line = line + jnp.where(lanes == c * TILE, 1.0, 0.0)
        table.append(line)
    for k in range(BASES):
        at = k * TILE
        pivot = table[k]
        inverse = 1.0 / jnp.broadcast_to(pivot[:, at : at + 1], pivot.shape)
        for c in range(k + 1, BASES + 1):
            ratio = jnp.broadcast_to(table[c][:, at : at + 1], pivot.shape) * inverse
            table[c] = jnp.where(lanes == at, ratio, table[c] - pivot * ratio)
    spread = table[BASES]
    for step in (1, 2, 4, 8):
        spread = spread + pltpu.roll(spread, step, 1)
    line = lax.broadcasted_iota(jnp.int32, (TILE, 128), 0)
    lane = lax.broadcasted_iota(jnp.int32, (TILE, 128), 1)
    same = (line == lane % TILE) & (lane < BASES * TILE)
    order_copy.wait()
    copies = []
    for slot in range(slots):
        blocks = [
            jnp.where(same, spread[slot * cap + k : slot * cap + k + 1, :], 0.0) for k in range(cap)
        ]
        exact = jnp.concatenate(blocks, axis=0)[:, : BASES * TILE]
        high = exact.astype(jnp.bfloat16)
        low = (exact - high.astype(jnp.float32)).astype(jnp.bfloat16)
        basis = basis_ref[slot]
        fitted = jnp.dot(high, basis, preferred_element_type=jnp.float32) + jnp.dot(
            low, basis, preferred_element_type=jnp.float32
        )
        for k in range(cap):
            j = order_ref[slot * cap + k]
            place = slot * cap + k
            for g in range(tiles):
                part = fitted[k * TILE : (k + 1) * TILE, g * cols : (g + 1) * cols]
                image = image_ref[j, g * TILE : (g + 1) * TILE, :].astype(jnp.float32)
                difference_ref[place, g * TILE : (g + 1) * TILE, :] = (image - part).astype(jnp.bfloat16)
            copy = pltpu.make_async_copy(difference_ref.at[place], difference_hbm.at[j], sem.at[place])
            copy.start()
            copies.append(copy)
    for copy in copies:
        copy.wait()


def call(kernel, name, outs, in_specs, out_specs, args, scratch=(), flops=0, size=0, limit=VMEM_LIMIT):
    return pl.pallas_call(
        kernel,
        out_shape=outs,
        in_specs=in_specs,
        out_specs=out_specs,
        scratch_shapes=list(scratch),
        name=name,
        compiler_params=pltpu.CompilerParams(vmem_limit_bytes=limit),
        cost_estimate=pl.CostEstimate(flops=flops, bytes_accessed=size, transcendentals=0),
    )(*args)


def body(images, mask_bits, visit_weight, intersection, patch_owner):
    visits = lax.axis_size("visit")
    strips = lax.axis_size("strip")
    _, pieces, rows, cols = images.shape
    slots = visits // 2
    cap = pieces // slots
    tiles = rows // TILE
    shape = jax.ShapeDtypeStruct
    bf16, f32 = jnp.bfloat16, jnp.float32
    image = images[0]
    mask = mask_bits[0]
    halves = strips == 2 and visits == 4
    half = rows // 2 if halves else rows
    ids = intersection[:, 0]
    label_rows = -(-slots // TILE) * TILE
    message_rows = slots * 2 * half * (cols // LANES)
    message_shape = (label_rows + message_rows, LANES)

    message = call(
        functools.partial(first_kernel, slots, cap, half, halves),
        "first_sums",
        shape(message_shape, bf16),
        [HBM] * 4,
        HBM,
        (ids, visit_weight, image, mask),
        scratch=[
            pltpu.VMEM(message_shape, bf16),
            pltpu.SMEM((pieces,), jnp.int32),
            pltpu.SMEM((pieces,), f32),
            pltpu.SMEM((pieces,), jnp.int32),
            pltpu.VMEM((1, pieces), bf16),
            pltpu.VMEM((pieces, half, cols), bf16),
            pltpu.VMEM((pieces, half, cols), jnp.int32),
            pltpu.SemaphoreType.DMA((2,)),
            pltpu.SemaphoreType.DMA((half // TILE, 2)),
            pltpu.SemaphoreType.DMA((half // TILE,)),
        ],
        size=2 << 20,
        limit=FETCH_LIMIT,
    )

    sorted_shape = shape((slots, cap * TILE, tiles * cols), bf16)
    sorted_outs = (sorted_shape, sorted_shape, shape((pieces,), jnp.int32))
    if halves:

        shifts = sorted(range(1, visits), key=lambda shift: min(shift, visits - shift))

        def everyone(value):
            others = [
                lax.ppermute(value, "visit", [(i, i ^ shift) for i in range(visits)]) for shift in shifts
            ]
            return [value] + others

        firsts = everyone(message)
        second, usable, masked, order = call(
            functools.partial(second_kernel, slots, cap, half),
            "second_sums",
            (shape((message_rows, LANES), bf16), *sorted_outs),
            [SMEM] + [VMEM] * 3,
            (VMEM,) * 3 + (SMEM,),
            (ids, visit_weight, image, mask),
            scratch=[pltpu.SMEM((pieces,), f32)],
            size=3 << 20,
        )
        seconds = everyone(second)
    else:
        usable, masked, order = call(
            functools.partial(sort_kernel, slots, cap),
            "sorted_usable",
            sorted_outs,
            [SMEM, VMEM, VMEM],
            (VMEM, VMEM, SMEM),
            (ids, image, mask),
            size=3 << 20,
        )
    normal_outs = (shape((slots, BASES * TILE, tiles * cols), bf16), shape((pieces, 128), f32))
    normal_scratch = [
        pltpu.VMEM((3, slots, rows, cols), bf16),
        pltpu.VMEM(((BASES + 1) * cap * TILE, tiles * cols), bf16),
    ]
    across = jnp.asarray(across_matrices(cols))
    if halves:
        template, coadd, edge, mine = call(
            functools.partial(border_kernel, slots, visits, half),
            "border",
            (
                shape((slots, half, cols), bf16),
                shape((half, cols), bf16),
                shape((slots, TILE, cols), bf16),
                shape((8, LANES), f32),
            ),
            [SMEM] + [VMEM] * visits,
            (VMEM,) * 4,
            (patch_owner, *firsts),
            size=1 << 20,
        )
        halo = lax.ppermute(edge, "strip", [(0, 1), (1, 0)])
        low, high = list(range(half)), list(range(half, rows))
        vertical = np.stack(
            [
                vertical_matrix(rows, high + low + list(range(rows, rows + TILE))),
                vertical_matrix(rows, low + high + list(range(-TILE, 0))),
            ]
        )
        basis, sums, coadd = call(
            functools.partial(halves_kernel, slots, cap, visits, half),
            "normal_equations",
            (*normal_outs, shape((rows, cols), bf16)),
            [VMEM] * (2 * visits + 8),
            (VMEM,) * 3,
            (
                mine,
                *firsts,
                *seconds,
                template,
                halo,
                coadd,
                jnp.asarray(vertical),
                across,
                usable,
                masked,
            ),
            scratch=[pltpu.VMEM((slots, half, cols), bf16)] + normal_scratch,
            size=2 << 20,
        )
        totals = [sums, lax.ppermute(sums, "strip", [(0, 1), (1, 0)])]
    else:
        template, coadd, edge = call(
            functools.partial(gathered_kernel, slots),
            "combine",
            (shape((slots, rows, cols), bf16), shape((rows, cols), bf16), shape((slots, 2 * TILE, cols), bf16)),
            [SMEM, VMEM],
            (VMEM,) * 3,
            (patch_owner, lax.all_gather(message, "visit")),
            scratch=[pltpu.VMEM((slots + 1, 2, rows, cols), f32)],
            size=1 << 20,
        )
        below = lax.ppermute(edge[:, TILE:], "strip", [(i, i + 1) for i in range(strips - 1)])
        above = lax.ppermute(edge[:, :TILE], "strip", [(i + 1, i) for i in range(strips - 1)])
        around = list(range(rows)) + list(range(-TILE, 0)) + list(range(rows, rows + TILE))
        basis, sums = call(
            functools.partial(normal_kernel, slots, cap),
            "normal_equations",
            normal_outs,
            [VMEM] * 7,
            (VMEM, VMEM),
            (template, below, above, jnp.asarray(vertical_matrix(rows, around)[None]), across, usable, masked),
            scratch=normal_scratch,
            size=2 << 20,
        )
        totals = [lax.psum(sums, "strip")]
    difference = call(
        functools.partial(fit_kernel, slots, cap),
        "fit",
        shape((pieces, rows, cols), bf16),
        [ANY] + [VMEM] * (len(totals) + 2),
        HBM,
        (order, *totals, basis, image),
        scratch=[
            pltpu.VMEM((pieces, rows, cols), bf16),
            pltpu.SMEM((pieces,), jnp.int32),
            pltpu.SemaphoreType.DMA((1,)),
            pltpu.SemaphoreType.DMA((pieces,)),
        ],
        size=2 << 20,
    )
    return (coadd[None, None], difference[None])


def solution(mesh):
    in_specs = (
        P("band", ("groups", "visit"), "strip", None),
        P("band", ("groups", "visit"), "strip", None),
        P("band", ("groups", "visit")),
        P(("groups", "visit"), None),
        P("groups"),
    )
    out_specs = (
        P("band", ("groups", "visit"), "strip", None),
        P("band", ("groups", "visit"), "strip", None),
    )
    return jax.shard_map(body, mesh=mesh, in_specs=in_specs, out_specs=out_specs, check_vma=False)
```

```python
import functools

import jax
import jax.numpy as jnp
import ml_dtypes
import numpy as np
from jax import lax
from jax.experimental import pallas as pl
from jax.experimental.pallas import tpu as pltpu
from jax.sharding import PartitionSpec as P

BASES = 6
HALF = 9
TILE = 16
LANES = 128
basis_rows = (0, 0, 1, 0, 2, 1)
basis_cols = (0, 1, 0, 2, 0, 1)
VMEM_LIMIT = 48 * 1024 * 1024
FETCH_LIMIT = 56 * 1024 * 1024

VMEM = pl.BlockSpec(memory_space=pltpu.VMEM)
SMEM = pl.BlockSpec(memory_space=pltpu.SMEM)
HBM = pl.BlockSpec(memory_space=pltpu.HBM)
ANY = pl.BlockSpec(memory_space=pl.ANY)


def tap_rows():
    offsets = np.arange(2 * HALF + 1).astype(np.float64) - HALF
    gaussian = np.exp(-offsets * offsets / 18.0)
    squared = gaussian * gaussian
    centre = np.sum(offsets * offsets * squared) / np.sum(squared)
    table = np.stack([gaussian, offsets * gaussian, (offsets * offsets - centre) * gaussian])
    table = table / np.sqrt(np.sum(table * table, axis=1, keepdims=True))
    return table.astype(ml_dtypes.bfloat16)


def across_matrices(cols):
    taps = tap_rows()
    distance = np.arange(cols)[:, None] - np.arange(cols)[None, :] + HALF
    inside = (distance >= 0) & (distance <= 2 * HALF)
    return np.where(inside[None], taps[:, np.clip(distance, 0, 2 * HALF)], 0).astype(ml_dtypes.bfloat16)


def vertical_matrix(rows, sources):
    taps = tap_rows()
    distance = np.asarray(sources)[None, :] - np.arange(rows)[:, None] + HALF
    inside = (distance >= 0) & (distance <= 2 * HALF)
    table = np.where(inside[None], taps[:, np.clip(distance, 0, 2 * HALF)], 0)
    return table.reshape(3 * rows, len(sources)).astype(ml_dtypes.bfloat16)


def unusable(mask):
    return jnp.bitwise_and(mask, 3) == 3


def piece_order(ids_ref, order_ref):
    pieces = order_ref.shape[0]
    ids = [ids_ref[j] for j in range(pieces)]
    for j in range(pieces):
        place = jnp.int32(0)
        for i in range(pieces):
            if i < j:
                place = place + (ids[i] <= ids[j]).astype(jnp.int32)
            elif i > j:
                place = place + (ids[i] < ids[j]).astype(jnp.int32)
        order_ref[place] = j


def piece_weights(weight_ref, splat_ref):
    weights = weight_ref[...].astype(jnp.float32)
    for j in range(splat_ref.shape[0]):
        splat_ref[j] = weights[0, j]


def windows(half, halves):
    if not halves:
        return 0, 0
    strip = lax.axis_index("strip")
    return pl.multiple_of((1 - strip) * half, TILE), pl.multiple_of(strip * half, TILE)


def put_sums(slots, cap, order_ref, weight_ref, image_of, mask_of, message_ref, base):
    cols = image_of(0).shape[1]
    parts = cols // LANES
    for slot in range(slots):
        numerator = jnp.zeros((TILE, cols), jnp.float32)
        denominator = jnp.zeros((TILE, cols), jnp.float32)
        for k in range(cap):
            j = order_ref[slot * cap + k]
            weight = jnp.where(unusable(mask_of(j)), 0.0, weight_ref[j])
            denominator = denominator + weight
            numerator = numerator + weight * image_of(j).astype(jnp.float32)
        for kind, value in enumerate((numerator.astype(jnp.bfloat16), denominator.astype(jnp.bfloat16))):
            for part in range(parts):
                at = base + ((slot * 2 + kind) * parts + part) * TILE
                message_ref[at : at + TILE, :] = value[:, part * LANES : (part + 1) * LANES]


def first_kernel(slots, cap, half, halves, ids_hbm, weight_hbm, image_hbm, mask_hbm, message_hbm, *refs):
    message_ref, order_ref, splat_ref, ids_ref, weight_ref, image_ref, mask_ref, small_sem, sem, out_sem = refs
    tiles = half // TILE
    step = slots * 2 * TILE * (image_ref.shape[2] // LANES)
    first = windows(half, halves)[0]
    small = [
        pltpu.make_async_copy(ids_hbm, ids_ref, small_sem.at[0]),
        pltpu.make_async_copy(weight_hbm, weight_ref, small_sem.at[1]),
    ]
    large = []
    for g in range(tiles):
        source = pl.ds(first + g * TILE, TILE)
        here = slice(g * TILE, (g + 1) * TILE)
        large.append(
            (
                pltpu.make_async_copy(mask_hbm.at[:, source, :], mask_ref.at[:, here, :], sem.at[g, 0]),
                pltpu.make_async_copy(image_hbm.at[:, source, :], image_ref.at[:, here, :], sem.at[g, 1]),
            )
        )
    for copy in small:
        copy.start()
    for pair in large:
        for copy in pair:
            copy.start()
    for copy in small:
        copy.wait()
    piece_order(ids_ref, order_ref)
    piece_weights(weight_ref, splat_ref)
    label_rows = message_ref.shape[0] - tiles * step
    line = lax.broadcasted_iota(jnp.int32, (label_rows, LANES), 0)
    labels = jnp.zeros((label_rows, LANES), jnp.float32)
    for slot in range(slots):
        labels = jnp.where(line == slot, ids_ref[order_ref[slot * cap]].astype(jnp.float32), labels)
    message_ref[:label_rows, :] = labels.astype(jnp.bfloat16)
    done, copies = 0, []
    for g in range(tiles):
        for copy in large[g]:
            copy.wait()
        here = slice(g * TILE, (g + 1) * TILE)
        base = label_rows + g * step
        put_sums(
            slots,
            cap,
            order_ref,
            splat_ref,
            lambda j, here=here: image_ref[j, here, :],
            lambda j, here=here: mask_ref[j, here, :],
            message_ref,
            base,
        )
        ready = pl.ds(done, base + step - done)
        copies.append(pltpu.make_async_copy(message_ref.at[ready, :], message_hbm.at[ready, :], out_sem.at[g]))
        copies[-1].start()
        done = base + step
    for copy in copies:
        copy.wait()


def second_kernel(slots, cap, half, ids_ref, weight_ref, image_ref, mask_ref, *refs):
    message_ref, usable_ref, masked_ref, order_ref, splat_ref = refs
    first = windows(half, True)[1]
    step = slots * 2 * TILE * (image_ref.shape[2] // LANES)
    piece_order(ids_ref, order_ref)
    piece_weights(weight_ref, splat_ref)
    for g in range(half // TILE):
        here = pl.ds(first + g * TILE, TILE)
        put_sums(
            slots,
            cap,
            order_ref,
            splat_ref,
            lambda j, here=here: image_ref[j, here, :],
            lambda j, here=here: mask_ref[j, here, :],
            message_ref,
            g * step,
        )
    put_sorted(slots, cap, order_ref, image_ref, mask_ref, usable_ref, masked_ref)


def sort_kernel(slots, cap, ids_ref, image_ref, mask_ref, usable_ref, masked_ref, order_ref):
    piece_order(ids_ref, order_ref)
    put_sorted(slots, cap, order_ref, image_ref, mask_ref, usable_ref, masked_ref)


def put_sorted(slots, cap, order_ref, image_ref, mask_ref, usable_ref, masked_ref):
    rows, cols = image_ref.shape[1:]
    for slot in range(slots):
        for k in range(cap):
            j = order_ref[slot * cap + k]
            for g in range(rows // TILE):
                lines = slice(g * TILE, (g + 1) * TILE)
                usable = jnp.where(unusable(mask_ref[j, lines, :]), 0.0, 1.0).astype(jnp.bfloat16)
                at = (slot, slice(k * TILE, (k + 1) * TILE), slice(g * cols, (g + 1) * cols))
                usable_ref[at] = usable
                masked_ref[at] = usable * image_ref[j, lines, :]


def owned_patch(owner_ref):
    visit = lax.axis_index("visit")
    mine = jnp.int32(0)
    for p in range(owner_ref.shape[0]):
        mine = jnp.where(owner_ref[p] == visit, p, mine)
    return mine.astype(jnp.float32)


def picks(labels, own_labels, mine, slots, slot):
    label = labels[slot : slot + 1, :]
    hits = [label == own_labels[t : t + 1, :] for t in range(slots)]
    if mine is not None:
        hits.append(label == mine)
    return [hit.astype(jnp.float32) for hit in hits]


def quotient(numerator, denominator):
    return (numerator / jnp.maximum(denominator, 1.0)).astype(jnp.bfloat16)


def combine(slots, rows, cols, base, mine, labels, sources, put):
    parts = cols // LANES
    labels = [value.astype(jnp.float32) for value in labels]
    hits = [[picks(label, labels[0], mine, slots, slot) for slot in range(slots)] for label in labels]
    targets = range(slots) if mine is None else range(slots, slots + 1)
    for first in range(0, rows, TILE):
        for part in range(parts):
            sums = [[jnp.zeros((TILE, LANES), jnp.float32) for _ in range(2)] for _ in range(slots + 1)]
            for d, ref in enumerate(sources):
                for slot in range(slots):
                    for kind in range(2):
                        at = base + (first * slots * 2 + (slot * 2 + kind) * TILE) * parts + part * TILE
                        value = ref[at : at + TILE, :].astype(jnp.float32)
                        for t in targets:
                            if d == 0 and t < slots:
                                if t == slot:
                                    sums[t][kind] = sums[t][kind] + value
                            else:
                                sums[t][kind] = sums[t][kind] + hits[d][slot][t] * value
            lanes = slice(part * LANES, (part + 1) * LANES)
            for t in targets:
                put(t, first, lanes, quotient(*sums[t]))


def message_base(ref, slots, rows, cols):
    return ref.shape[0] - slots * 2 * rows * (cols // LANES)


def border_kernel(slots, rows, *refs):
    sources, (template_ref, edge_ref) = refs[:-2], refs[-2:]
    cols = template_ref.shape[2]
    base = message_base(sources[0], slots, rows, cols)

    def put(t, first, lanes, value):
        template_ref[t, first : first + TILE, lanes] = value

    combine(slots, rows, cols, base, None, [ref[:base, :] for ref in sources], sources, put)
    at = pl.multiple_of((1 - lax.axis_index("strip")) * (rows - TILE), TILE)
    edge_ref[...] = template_ref[:, pl.ds(at, TILE), :]


def own_kernel(slots, count, rows, owner_ref, after_ref, *refs):
    firsts, seconds, coadd_ref = refs[:count], refs[count : 2 * count], refs[2 * count]
    del after_ref
    cols = coadd_ref.shape[1]
    base = message_base(firsts[0], slots, rows, cols)
    labels = [ref[:base, :] for ref in firsts]
    mine = owned_patch(owner_ref)
    for sources, skip, start in zip((firsts, seconds), (base, 0), windows(rows, True)):

        def put(t, first, lanes, value, start=start):
            coadd_ref[pl.ds(start + first, TILE), lanes] = value

        combine(slots, rows, cols, skip, mine, labels, sources, put)


def gathered_kernel(slots, owner_ref, stacked_ref, template_ref, coadd_ref, edge_ref, total_ref):
    rows, cols = coadd_ref.shape
    parts = cols // LANES
    base = stacked_ref.shape[1] - rows * slots * 2 * parts
    mine = owned_patch(owner_ref)
    own_labels = stacked_ref[lax.axis_index("visit"), :base, :].astype(jnp.float32)
    total_ref[...] = jnp.zeros_like(total_ref)

    def add_source(d, carry):
        labels = stacked_ref[d, :base, :].astype(jnp.float32)
        for slot in range(slots):
            pick = picks(labels, own_labels, mine, slots, slot)
            for kind in range(2):
                for first in range(0, rows, TILE):
                    for part in range(parts):
                        at = base + (first * slots * 2 + (slot * 2 + kind) * TILE) * parts + part * TILE
                        value = stacked_ref[d, at : at + TILE, :].astype(jnp.float32)
                        lanes = slice(part * LANES, (part + 1) * LANES)
                        for t in range(slots + 1):
                            total_ref[t, kind, first : first + TILE, lanes] += pick[t] * value
        return carry

    lax.fori_loop(0, stacked_ref.shape[0], add_source, 0)
    for t in range(slots):
        template_ref[t] = quotient(total_ref[t, 0], total_ref[t, 1])
    coadd_ref[...] = quotient(total_ref[slots, 0], total_ref[slots, 1])
    edge_ref[:, :TILE, :] = template_ref[:, :TILE, :]
    edge_ref[:, TILE:, :] = template_ref[:, rows - TILE :, :]


def halves_kernel(slots, cap, count, rows, *refs):
    firsts, seconds, refs = refs[:count], refs[count : 2 * count], refs[2 * count :]
    template_ref, halo_ref, vertical_ref, across_ref, usable_ref, masked_ref = refs[:6]
    basis_ref, sums_ref, second_ref, smooth_ref, left_ref = refs[6:]
    cols = template_ref.shape[2]
    base = message_base(firsts[0], slots, rows, cols)

    def put(t, first, lanes, value):
        second_ref[t, first : first + TILE, lanes] = value

    combine(slots, rows, cols, 0, None, [ref[:base, :] for ref in firsts], seconds, put)
    normal_equations(
        slots,
        cap,
        [template_ref, second_ref, halo_ref],
        vertical_ref[lax.axis_index("strip")],
        across_ref,
        usable_ref,
        masked_ref,
        basis_ref,
        sums_ref,
        smooth_ref,
        left_ref,
    )


def normal_kernel(slots, cap, template_ref, below_ref, above_ref, vertical_ref, *refs):
    normal_equations(slots, cap, [template_ref, below_ref, above_ref], vertical_ref[0], *refs)


def normal_equations(
    slots, cap, parts, vertical, across_ref, usable_ref, masked_ref, basis_ref, sums_ref, smooth_ref, left_ref
):
    rows, cols = smooth_ref.shape[2:]
    tiles = rows // TILE
    for slot in range(slots):
        extended = jnp.concatenate([ref[slot] for ref in parts], axis=0)
        smooth = jnp.dot(vertical, extended, preferred_element_type=jnp.float32)
        for k in range(3):
            smooth_ref[k, slot] = smooth[k * rows : (k + 1) * rows].astype(jnp.bfloat16)
    for c in range(3):
        users = [a for a in range(BASES) if basis_cols[a] == c]
        for slot in range(slots):
            stacked = jnp.concatenate([smooth_ref[basis_rows[a], slot] for a in users], axis=0)
            planes = jnp.dot(stacked, across_ref[c], preferred_element_type=jnp.float32).astype(jnp.bfloat16)
            for n, a in enumerate(users):
                for g in range(tiles):
                    at = n * rows + g * TILE
                    basis_ref[slot, a * TILE : (a + 1) * TILE, g * cols : (g + 1) * cols] = planes[at : at + TILE]
    group = cap * TILE
    height = BASES * group + group
    for slot in range(slots):
        for a in range(BASES):
            plane = basis_ref[slot, a * TILE : (a + 1) * TILE, :]
            for k in range(cap):
                at = a * group + k * TILE
                left_ref[at : at + TILE, :] = plane * usable_ref[slot, k * TILE : (k + 1) * TILE, :]
        left_ref[BASES * group :, :] = masked_ref[slot]
        product = lax.dot_general(
            left_ref[...], basis_ref[slot], (((1,), (1,)), ((), ())), preferred_element_type=jnp.float32
        )
        width = product.shape[1]
        line = lax.broadcasted_iota(jnp.int32, (TILE, width), 0)
        lane = lax.broadcasted_iota(jnp.int32, (TILE, width), 1)
        same = line == lane % TILE
        product = jnp.where(same[None], product.reshape(height // TILE, TILE, width), 0.0)
        product = jnp.sum(product, axis=1)
        product = jnp.concatenate([product, jnp.zeros((height // TILE, 128 - width), jnp.float32)], axis=1)
        for step in (1, 2, 4, 8):
            product = product + pltpu.roll(product, 128 - step, 1)
        lanes = lax.broadcasted_iota(jnp.int32, product.shape, 1)
        product = jnp.where(lanes % TILE == 0, product, 0.0)
        packed = product[:cap]
        for a in range(1, BASES + 1):
            packed = packed + pltpu.roll(product[a * cap : (a + 1) * cap], a, 1)
        sums_ref[slot * cap : (slot + 1) * cap, :] = packed


def fit_kernel(slots, cap, order_any, *refs):
    sums_refs, refs = refs[:-7], refs[-7:]
    basis_ref, image_ref, difference_hbm, difference_ref, order_ref, order_sem, sem = refs
    order_copy = pltpu.make_async_copy(order_any, order_ref, order_sem.at[0])
    order_copy.start()
    rows, cols = image_ref.shape[1:]
    tiles = rows // TILE
    total = sums_refs[0][...]
    for ref in sums_refs[1:]:
        total = total + ref[...]
    pieces = total.shape[0]
    lanes = lax.broadcasted_iota(jnp.int32, (pieces, 128), 1)
    starts = lanes % TILE == 0
    table = []
    for c in range(BASES + 1):
        line = total if c == 0 else pltpu.roll(total, 128 - c, 1)
        line = jnp.where(starts, line, 0.0)
        if c < BASES:
            line = line + jnp.where(lanes == c * TILE, 1.0, 0.0)
        table.append(line)
    def entry(line, a):
        return jnp.broadcast_to(line[:, a * TILE : a * TILE + 1], line.shape)

    for k in range(0, BASES, 2):
        first, second = table[k], table[k + 1]
        p, q, r, s = entry(first, k), entry(second, k), entry(first, k + 1), entry(second, k + 1)
        inverse = 1.0 / (p * s - q * r)
        for c in range(k + 2, BASES + 1):
            above, below = entry(table[c], k), entry(table[c], k + 1)
            x = (s * above - q * below) * inverse
            y = (p * below - r * above) * inverse
            rest = table[c] - (first * x + second * y)
            table[c] = jnp.where(lanes == k * TILE, x, jnp.where(lanes == (k + 1) * TILE, y, rest))
    exact = [entry(table[BASES], a) for a in range(BASES)]
    high = [value.astype(jnp.bfloat16).astype(jnp.float32) for value in exact]
    terms = high + [value - upper for value, upper in zip(exact, high)]
    group = lanes // TILE
    spread = []
    for first in range(0, len(terms), LANES // TILE):
        several = terms[first : first + LANES // TILE]
        line = several[0]
        for g in range(1, len(several)):
            line = jnp.where(group >= g, several[g], line)
        spread.append(line)
    width = len(terms) * TILE
    spread = jnp.concatenate(spread, axis=1)[:, :width]
    line = lax.broadcasted_iota(jnp.int32, (TILE, width), 0)
    lane = lax.broadcasted_iota(jnp.int32, (TILE, width), 1)
    same = line == lane % TILE
    order_copy.wait()
    copies = []
    for slot in range(slots):
        blocks = [
            jnp.where(same, spread[slot * cap + k : slot * cap + k + 1, :], 0.0).astype(jnp.bfloat16)
            for k in range(cap)
        ]
        basis = basis_ref[slot]
        fitted = jnp.dot(
            jnp.concatenate(blocks, axis=0),
            jnp.concatenate([basis, basis], axis=0),
            preferred_element_type=jnp.float32,
        )
        for k in range(cap):
            j = order_ref[slot * cap + k]
            place = slot * cap + k
            for g in range(tiles):
                part = fitted[k * TILE : (k + 1) * TILE, g * cols : (g + 1) * cols]
                image = image_ref[j, g * TILE : (g + 1) * TILE, :].astype(jnp.float32)
                difference_ref[place, g * TILE : (g + 1) * TILE, :] = (image - part).astype(jnp.bfloat16)
            copy = pltpu.make_async_copy(difference_ref.at[place], difference_hbm.at[j], sem.at[place])
            copy.start()
            copies.append(copy)
    for copy in copies:
        copy.wait()


def call(kernel, name, outs, in_specs, out_specs, args, scratch=(), flops=0, size=0, limit=VMEM_LIMIT):
    return pl.pallas_call(
        kernel,
        out_shape=outs,
        in_specs=in_specs,
        out_specs=out_specs,
        scratch_shapes=list(scratch),
        name=name,
        compiler_params=pltpu.CompilerParams(vmem_limit_bytes=limit),
        cost_estimate=pl.CostEstimate(flops=flops, bytes_accessed=size, transcendentals=0),
    )(*args)


def body(images, mask_bits, visit_weight, intersection, patch_owner):
    visits = lax.axis_size("visit")
    strips = lax.axis_size("strip")
    _, pieces, rows, cols = images.shape
    slots = visits // 2
    cap = pieces // slots
    tiles = rows // TILE
    shape = jax.ShapeDtypeStruct
    bf16, f32 = jnp.bfloat16, jnp.float32
    image = images[0]
    mask = mask_bits[0]
    halves = strips == 2 and visits == 4
    half = rows // 2 if halves else rows
    ids = intersection[:, 0]
    label_rows = -(-slots // TILE) * TILE
    message_rows = slots * 2 * half * (cols // LANES)
    message_shape = (label_rows + message_rows, LANES)

    message = call(
        functools.partial(first_kernel, slots, cap, half, halves),
        "first_sums",
        shape(message_shape, bf16),
        [HBM] * 4,
        HBM,
        (ids, visit_weight, image, mask),
        scratch=[
            pltpu.VMEM(message_shape, bf16),
            pltpu.SMEM((pieces,), jnp.int32),
            pltpu.SMEM((pieces,), f32),
            pltpu.SMEM((pieces,), jnp.int32),
            pltpu.VMEM((1, pieces), bf16),
            pltpu.VMEM((pieces, half, cols), bf16),
            pltpu.VMEM((pieces, half, cols), jnp.int32),
            pltpu.SemaphoreType.DMA((2,)),
            pltpu.SemaphoreType.DMA((half // TILE, 2)),
            pltpu.SemaphoreType.DMA((half // TILE,)),
        ],
        size=2 << 20,
        limit=FETCH_LIMIT,
    )

    sorted_shape = shape((slots, cap * TILE, tiles * cols), bf16)
    sorted_outs = (sorted_shape, sorted_shape, shape((pieces,), jnp.int32))
    if halves:

        shifts = sorted(range(1, visits), key=lambda shift: min(shift, visits - shift))

        def everyone(value):
            others = [
                lax.ppermute(value, "visit", [(i, i ^ shift) for i in range(visits)]) for shift in shifts
            ]
            return [value] + others

        firsts = everyone(message)
        second, usable, masked, order = call(
            functools.partial(second_kernel, slots, cap, half),
            "second_sums",
            (shape((message_rows, LANES), bf16), *sorted_outs),
            [SMEM] + [VMEM] * 3,
            (VMEM,) * 3 + (SMEM,),
            (ids, visit_weight, image, mask),
            scratch=[pltpu.SMEM((pieces,), f32)],
            size=3 << 20,
        )
        seconds = everyone(second)
    else:
        usable, masked, order = call(
            functools.partial(sort_kernel, slots, cap),
            "sorted_usable",
            sorted_outs,
            [SMEM, VMEM, VMEM],
            (VMEM, VMEM, SMEM),
            (ids, image, mask),
            size=3 << 20,
        )
    normal_outs = (shape((slots, BASES * TILE, tiles * cols), bf16), shape((pieces, 128), f32))
    normal_scratch = [
        pltpu.VMEM((3, slots, rows, cols), bf16),
        pltpu.VMEM(((BASES + 1) * cap * TILE, tiles * cols), bf16),
    ]
    across = jnp.asarray(across_matrices(cols))
    if halves:
        template, edge = call(
            functools.partial(border_kernel, slots, half),
            "border",
            (shape((slots, half, cols), bf16), shape((slots, TILE, cols), bf16)),
            [VMEM] * visits,
            (VMEM,) * 2,
            firsts,
            size=1 << 20,
        )
        halo = lax.ppermute(edge, "strip", [(0, 1), (1, 0)])
        low, high = list(range(half)), list(range(half, rows))
        vertical = np.stack(
            [
                vertical_matrix(rows, high + low + list(range(rows, rows + TILE))),
                vertical_matrix(rows, low + high + list(range(-TILE, 0))),
            ]
        )
        basis, sums = call(
            functools.partial(halves_kernel, slots, cap, visits, half),
            "normal_equations",
            normal_outs,
            [VMEM] * (2 * visits + 6),
            (VMEM,) * 2,
            (*firsts, *seconds, template, halo, jnp.asarray(vertical), across, usable, masked),
            scratch=[pltpu.VMEM((slots, half, cols), bf16)] + normal_scratch,
            size=2 << 20,
        )
        coadd = call(
            functools.partial(own_kernel, slots, visits, half),
            "own_patch",
            shape((rows, cols), bf16),
            [SMEM, ANY] + [VMEM] * (2 * visits),
            VMEM,
            (patch_owner, sums, *firsts, *seconds),
            size=1 << 20,
        )
        totals = [sums, lax.ppermute(sums, "strip", [(0, 1), (1, 0)])]
    else:
        template, coadd, edge = call(
            functools.partial(gathered_kernel, slots),
            "combine",
            (shape((slots, rows, cols), bf16), shape((rows, cols), bf16), shape((slots, 2 * TILE, cols), bf16)),
            [SMEM, VMEM],
            (VMEM,) * 3,
            (patch_owner, lax.all_gather(message, "visit")),
            scratch=[pltpu.VMEM((slots + 1, 2, rows, cols), f32)],
            size=1 << 20,
        )
        below = lax.ppermute(edge[:, TILE:], "strip", [(i, i + 1) for i in range(strips - 1)])
        above = lax.ppermute(edge[:, :TILE], "strip", [(i + 1, i) for i in range(strips - 1)])
        around = list(range(rows)) + list(range(-TILE, 0)) + list(range(rows, rows + TILE))
        basis, sums = call(
            functools.partial(normal_kernel, slots, cap),
            "normal_equations",
            normal_outs,
            [VMEM] * 7,
            (VMEM, VMEM),
            (template, below, above, jnp.asarray(vertical_matrix(rows, around)[None]), across, usable, masked),
            scratch=normal_scratch,
            size=2 << 20,
        )
        totals = [lax.psum(sums, "strip")]
    difference = call(
        functools.partial(fit_kernel, slots, cap),
        "fit",
        shape((pieces, rows, cols), bf16),
        [ANY] + [VMEM] * (len(totals) + 2),
        HBM,
        (order, *totals, basis, image),
        scratch=[
            pltpu.VMEM((pieces, rows, cols), bf16),
            pltpu.SMEM((pieces,), jnp.int32),
            pltpu.SemaphoreType.DMA((1,)),
            pltpu.SemaphoreType.DMA((pieces,)),
        ],
        size=2 << 20,
    )
    return (coadd[None, None], difference[None])


def solution(mesh):
    in_specs = (
        P("band", ("groups", "visit"), "strip", None),
        P("band", ("groups", "visit"), "strip", None),
        P("band", ("groups", "visit")),
        P(("groups", "visit"), None),
        P("groups"),
    )
    out_specs = (
        P("band", ("groups", "visit"), "strip", None),
        P("band", ("groups", "visit"), "strip", None),
    )
    return jax.shard_map(body, mesh=mesh, in_specs=in_specs, out_specs=out_specs, check_vma=False)
```

```python
import functools

import jax
import jax.numpy as jnp
import ml_dtypes
import numpy as np
from jax import lax
from jax.experimental import pallas as pl
from jax.experimental.pallas import tpu as pltpu
from jax.sharding import PartitionSpec as P

BASES = 6
HALF = 9
TILE = 16
LANES = 128
basis_rows = (0, 0, 1, 0, 2, 1)
basis_cols = (0, 1, 0, 2, 0, 1)
VMEM_LIMIT = 48 * 1024 * 1024
FETCH_LIMIT = 56 * 1024 * 1024

VMEM = pl.BlockSpec(memory_space=pltpu.VMEM)
SMEM = pl.BlockSpec(memory_space=pltpu.SMEM)
HBM = pl.BlockSpec(memory_space=pltpu.HBM)
ANY = pl.BlockSpec(memory_space=pl.ANY)


def tap_rows():
    offsets = np.arange(2 * HALF + 1).astype(np.float64) - HALF
    gaussian = np.exp(-offsets * offsets / 18.0)
    squared = gaussian * gaussian
    centre = np.sum(offsets * offsets * squared) / np.sum(squared)
    table = np.stack([gaussian, offsets * gaussian, (offsets * offsets - centre) * gaussian])
    table = table / np.sqrt(np.sum(table * table, axis=1, keepdims=True))
    return table.astype(ml_dtypes.bfloat16)


def across_matrices(cols):
    taps = tap_rows()
    distance = np.arange(cols)[:, None] - np.arange(cols)[None, :] + HALF
    inside = (distance >= 0) & (distance <= 2 * HALF)
    return np.where(inside[None], taps[:, np.clip(distance, 0, 2 * HALF)], 0).astype(ml_dtypes.bfloat16)


def vertical_matrix(rows, sources):
    taps = tap_rows()
    distance = np.asarray(sources)[None, :] - np.arange(rows)[:, None] + HALF
    inside = (distance >= 0) & (distance <= 2 * HALF)
    table = np.where(inside[None], taps[:, np.clip(distance, 0, 2 * HALF)], 0)
    return table.reshape(3 * rows, len(sources)).astype(ml_dtypes.bfloat16)


def unusable(mask):
    return jnp.bitwise_and(mask, 3) == 3


def piece_order(ids_ref, order_ref):
    pieces = order_ref.shape[0]
    ids = [ids_ref[j] for j in range(pieces)]
    for j in range(pieces):
        place = jnp.int32(0)
        for i in range(pieces):
            if i < j:
                place = place + (ids[i] <= ids[j]).astype(jnp.int32)
            elif i > j:
                place = place + (ids[i] < ids[j]).astype(jnp.int32)
        order_ref[place] = j


def piece_weights(weight_ref, splat_ref):
    weights = weight_ref[...].astype(jnp.float32)
    for j in range(splat_ref.shape[0]):
        splat_ref[j] = weights[0, j]


def windows(half, halves):
    if not halves:
        return 0, 0
    strip = lax.axis_index("strip")
    return pl.multiple_of((1 - strip) * half, TILE), pl.multiple_of(strip * half, TILE)


def put_sums(slots, cap, order_ref, weight_ref, image_of, mask_of, message_ref, base):
    cols = image_of(0).shape[1]
    parts = cols // LANES
    for slot in range(slots):
        numerator = jnp.zeros((TILE, cols), jnp.float32)
        denominator = jnp.zeros((TILE, cols), jnp.float32)
        for k in range(cap):
            j = order_ref[slot * cap + k]
            weight = jnp.where(unusable(mask_of(j)), 0.0, weight_ref[j])
            denominator = denominator + weight
            numerator = numerator + weight * image_of(j).astype(jnp.float32)
        for kind, value in enumerate((numerator.astype(jnp.bfloat16), denominator.astype(jnp.bfloat16))):
            for part in range(parts):
                at = base + ((slot * 2 + kind) * parts + part) * TILE
                message_ref[at : at + TILE, :] = value[:, part * LANES : (part + 1) * LANES]


def first_kernel(slots, cap, half, halves, ids_hbm, weight_hbm, image_hbm, mask_hbm, message_hbm, *refs):
    message_ref, order_ref, splat_ref, ids_ref, weight_ref, image_ref, mask_ref, small_sem, sem, out_sem = refs
    tiles = half // TILE
    step = slots * 2 * TILE * (image_ref.shape[2] // LANES)
    first = windows(half, halves)[0]
    small = [
        pltpu.make_async_copy(ids_hbm, ids_ref, small_sem.at[0]),
        pltpu.make_async_copy(weight_hbm, weight_ref, small_sem.at[1]),
    ]
    large = []
    for g in range(tiles):
        source = pl.ds(first + g * TILE, TILE)
        here = slice(g * TILE, (g + 1) * TILE)
        large.append(
            (
                pltpu.make_async_copy(mask_hbm.at[:, source, :], mask_ref.at[:, here, :], sem.at[g, 0]),
                pltpu.make_async_copy(image_hbm.at[:, source, :], image_ref.at[:, here, :], sem.at[g, 1]),
            )
        )
    for copy in small:
        copy.start()
    for pair in large:
        for copy in pair:
            copy.start()
    for copy in small:
        copy.wait()
    piece_order(ids_ref, order_ref)
    piece_weights(weight_ref, splat_ref)
    label_rows = message_ref.shape[0] - tiles * step
    line = lax.broadcasted_iota(jnp.int32, (label_rows, LANES), 0)
    labels = jnp.zeros((label_rows, LANES), jnp.float32)
    for slot in range(slots):
        labels = jnp.where(line == slot, ids_ref[order_ref[slot * cap]].astype(jnp.float32), labels)
    message_ref[:label_rows, :] = labels.astype(jnp.bfloat16)
    done, copies = 0, []
    for g in range(tiles):
        for copy in large[g]:
            copy.wait()
        here = slice(g * TILE, (g + 1) * TILE)
        base = label_rows + g * step
        put_sums(
            slots,
            cap,
            order_ref,
            splat_ref,
            lambda j, here=here: image_ref[j, here, :],
            lambda j, here=here: mask_ref[j, here, :],
            message_ref,
            base,
        )
        ready = pl.ds(done, base + step - done)
        copies.append(pltpu.make_async_copy(message_ref.at[ready, :], message_hbm.at[ready, :], out_sem.at[g]))
        copies[-1].start()
        done = base + step
    for copy in copies:
        copy.wait()


def second_kernel(slots, cap, half, ids_ref, weight_ref, image_ref, mask_ref, *refs):
    message_ref, order_ref, splat_ref = refs
    first = windows(half, True)[1]
    step = slots * 2 * TILE * (image_ref.shape[2] // LANES)
    piece_order(ids_ref, order_ref)
    piece_weights(weight_ref, splat_ref)
    for g in range(half // TILE):
        here = pl.ds(first + g * TILE, TILE)
        put_sums(
            slots,
            cap,
            order_ref,
            splat_ref,
            lambda j, here=here: image_ref[j, here, :],
            lambda j, here=here: mask_ref[j, here, :],
            message_ref,
            g * step,
        )


def sort_kernel(slots, cap, ids_ref, image_ref, mask_ref, usable_ref, masked_ref, order_ref):
    piece_order(ids_ref, order_ref)
    put_sorted(slots, cap, order_ref, image_ref, mask_ref, usable_ref, masked_ref)


def put_sorted(slots, cap, order_ref, image_ref, mask_ref, usable_ref, masked_ref):
    rows, cols = image_ref.shape[1:]
    for slot in range(slots):
        for k in range(cap):
            j = order_ref[slot * cap + k]
            for g in range(rows // TILE):
                lines = slice(g * TILE, (g + 1) * TILE)
                usable = jnp.where(unusable(mask_ref[j, lines, :]), 0.0, 1.0).astype(jnp.bfloat16)
                at = (slot, slice(k * TILE, (k + 1) * TILE), slice(g * cols, (g + 1) * cols))
                usable_ref[at] = usable
                masked_ref[at] = usable * image_ref[j, lines, :]


def owned_patch(owner_ref):
    visit = lax.axis_index("visit")
    mine = jnp.int32(0)
    for p in range(owner_ref.shape[0]):
        mine = jnp.where(owner_ref[p] == visit, p, mine)
    return mine.astype(jnp.float32)


def picks(labels, own_labels, mine, slots, slot):
    label = labels[slot : slot + 1, :]
    hits = [label == own_labels[t : t + 1, :] for t in range(slots)]
    if mine is not None:
        hits.append(label == mine)
    return [hit.astype(jnp.float32) for hit in hits]


def quotient(numerator, denominator):
    return (numerator / jnp.maximum(denominator, 1.0)).astype(jnp.bfloat16)


def combine(slots, rows, cols, base, mine, labels, sources, put):
    parts = cols // LANES
    labels = [value.astype(jnp.float32) for value in labels]
    hits = [[picks(label, labels[0], mine, slots, slot) for slot in range(slots)] for label in labels]
    targets = range(slots) if mine is None else range(slots, slots + 1)
    for first in range(0, rows, TILE):
        for part in range(parts):
            sums = [[jnp.zeros((TILE, LANES), jnp.float32) for _ in range(2)] for _ in range(slots + 1)]
            for d, ref in enumerate(sources):
                for slot in range(slots):
                    for kind in range(2):
                        at = base + (first * slots * 2 + (slot * 2 + kind) * TILE) * parts + part * TILE
                        value = ref[at : at + TILE, :].astype(jnp.float32)
                        for t in targets:
                            if d == 0 and t < slots:
                                if t == slot:
                                    sums[t][kind] = sums[t][kind] + value
                            else:
                                sums[t][kind] = sums[t][kind] + hits[d][slot][t] * value
            lanes = slice(part * LANES, (part + 1) * LANES)
            for t in targets:
                put(t, first, lanes, quotient(*sums[t]))


def message_base(ref, slots, rows, cols):
    return ref.shape[0] - slots * 2 * rows * (cols // LANES)


def border_kernel(slots, rows, *refs):
    sources, (template_ref, edge_ref) = refs[:-2], refs[-2:]
    cols = template_ref.shape[2]
    base = message_base(sources[0], slots, rows, cols)

    def put(t, first, lanes, value):
        template_ref[t, first : first + TILE, lanes] = value

    combine(slots, rows, cols, base, None, [ref[:base, :] for ref in sources], sources, put)
    at = pl.multiple_of((1 - lax.axis_index("strip")) * (rows - TILE), TILE)
    edge_ref[...] = template_ref[:, pl.ds(at, TILE), :]


def own_kernel(slots, count, rows, owner_ref, after_ref, *refs):
    firsts, seconds, coadd_ref = refs[:count], refs[count : 2 * count], refs[2 * count]
    del after_ref
    cols = coadd_ref.shape[1]
    base = message_base(firsts[0], slots, rows, cols)
    labels = [ref[:base, :] for ref in firsts]
    mine = owned_patch(owner_ref)
    for sources, skip, start in zip((firsts, seconds), (base, 0), windows(rows, True)):

        def put(t, first, lanes, value, start=start):
            coadd_ref[pl.ds(start + first, TILE), lanes] = value

        combine(slots, rows, cols, skip, mine, labels, sources, put)


def gathered_kernel(slots, owner_ref, stacked_ref, template_ref, coadd_ref, edge_ref, total_ref):
    rows, cols = coadd_ref.shape
    parts = cols // LANES
    base = stacked_ref.shape[1] - rows * slots * 2 * parts
    mine = owned_patch(owner_ref)
    own_labels = stacked_ref[lax.axis_index("visit"), :base, :].astype(jnp.float32)
    total_ref[...] = jnp.zeros_like(total_ref)

    def add_source(d, carry):
        labels = stacked_ref[d, :base, :].astype(jnp.float32)
        for slot in range(slots):
            pick = picks(labels, own_labels, mine, slots, slot)
            for kind in range(2):
                for first in range(0, rows, TILE):
                    for part in range(parts):
                        at = base + (first * slots * 2 + (slot * 2 + kind) * TILE) * parts + part * TILE
                        value = stacked_ref[d, at : at + TILE, :].astype(jnp.float32)
                        lanes = slice(part * LANES, (part + 1) * LANES)
                        for t in range(slots + 1):
                            total_ref[t, kind, first : first + TILE, lanes] += pick[t] * value
        return carry

    lax.fori_loop(0, stacked_ref.shape[0], add_source, 0)
    for t in range(slots):
        template_ref[t] = quotient(total_ref[t, 0], total_ref[t, 1])
    coadd_ref[...] = quotient(total_ref[slots, 0], total_ref[slots, 1])
    edge_ref[:, :TILE, :] = template_ref[:, :TILE, :]
    edge_ref[:, TILE:, :] = template_ref[:, rows - TILE :, :]


def halves_kernel(slots, cap, count, rows, *refs):
    firsts, seconds, refs = refs[:count], refs[count : 2 * count], refs[2 * count :]
    template_ref, halo_ref, vertical_ref, across_ref, usable_ref, masked_ref = refs[:6]
    basis_ref, sums_ref, second_ref, smooth_ref, left_ref = refs[6:]
    cols = template_ref.shape[2]
    base = message_base(firsts[0], slots, rows, cols)

    def put(t, first, lanes, value):
        second_ref[t, first : first + TILE, lanes] = value

    combine(slots, rows, cols, 0, None, [ref[:base, :] for ref in firsts], seconds, put)
    normal_equations(
        slots,
        cap,
        [template_ref, second_ref, halo_ref],
        vertical_ref[lax.axis_index("strip")],
        across_ref,
        usable_ref,
        masked_ref,
        basis_ref,
        sums_ref,
        smooth_ref,
        left_ref,
    )


def normal_kernel(slots, cap, template_ref, below_ref, above_ref, vertical_ref, *refs):
    normal_equations(slots, cap, [template_ref, below_ref, above_ref], vertical_ref[0], *refs)


def normal_equations(
    slots, cap, parts, vertical, across_ref, usable_ref, masked_ref, basis_ref, sums_ref, smooth_ref, left_ref
):
    rows, cols = smooth_ref.shape[2:]
    tiles = rows // TILE
    for slot in range(slots):
        extended = jnp.concatenate([ref[slot] for ref in parts], axis=0)
        smooth = jnp.dot(vertical, extended, preferred_element_type=jnp.float32)
        for k in range(3):
            smooth_ref[k, slot] = smooth[k * rows : (k + 1) * rows].astype(jnp.bfloat16)
    for c in range(3):
        users = [a for a in range(BASES) if basis_cols[a] == c]
        for slot in range(slots):
            stacked = jnp.concatenate([smooth_ref[basis_rows[a], slot] for a in users], axis=0)
            planes = jnp.dot(stacked, across_ref[c], preferred_element_type=jnp.float32).astype(jnp.bfloat16)
            for n, a in enumerate(users):
                for g in range(tiles):
                    at = n * rows + g * TILE
                    basis_ref[slot, a * TILE : (a + 1) * TILE, g * cols : (g + 1) * cols] = planes[at : at + TILE]
    group = cap * TILE
    height = BASES * group + group
    for slot in range(slots):
        for a in range(BASES):
            plane = basis_ref[slot, a * TILE : (a + 1) * TILE, :]
            for k in range(cap):
                at = a * group + k * TILE
                left_ref[at : at + TILE, :] = plane * usable_ref[slot, k * TILE : (k + 1) * TILE, :]
        left_ref[BASES * group :, :] = masked_ref[slot]
        product = lax.dot_general(
            left_ref[...], basis_ref[slot], (((1,), (1,)), ((), ())), preferred_element_type=jnp.float32
        )
        width = product.shape[1]
        line = lax.broadcasted_iota(jnp.int32, (TILE, width), 0)
        lane = lax.broadcasted_iota(jnp.int32, (TILE, width), 1)
        same = line == lane % TILE
        product = jnp.where(same[None], product.reshape(height // TILE, TILE, width), 0.0)
        product = jnp.sum(product, axis=1)
        product = jnp.concatenate([product, jnp.zeros((height // TILE, 128 - width), jnp.float32)], axis=1)
        for step in (1, 2, 4, 8):
            product = product + pltpu.roll(product, 128 - step, 1)
        lanes = lax.broadcasted_iota(jnp.int32, product.shape, 1)
        product = jnp.where(lanes % TILE == 0, product, 0.0)
        packed = product[:cap]
        for a in range(1, BASES + 1):
            packed = packed + pltpu.roll(product[a * cap : (a + 1) * cap], a, 1)
        sums_ref[slot * cap : (slot + 1) * cap, :] = packed


def fit_kernel(slots, cap, order_any, *refs):
    sums_refs, refs = refs[:-7], refs[-7:]
    basis_ref, image_ref, difference_hbm, difference_ref, order_ref, order_sem, sem = refs
    order_copy = pltpu.make_async_copy(order_any, order_ref, order_sem.at[0])
    order_copy.start()
    rows, cols = image_ref.shape[1:]
    tiles = rows // TILE
    total = sums_refs[0][...]
    for ref in sums_refs[1:]:
        total = total + ref[...]
    pieces = total.shape[0]
    lanes = lax.broadcasted_iota(jnp.int32, (pieces, 128), 1)
    starts = lanes % TILE == 0
    table = []
    for c in range(BASES + 1):
        line = total if c == 0 else pltpu.roll(total, 128 - c, 1)
        line = jnp.where(starts, line, 0.0)
        if c < BASES:
            line = line + jnp.where(lanes == c * TILE, 1.0, 0.0)
        table.append(line)
    def entry(line, a):
        return jnp.broadcast_to(line[:, a * TILE : a * TILE + 1], line.shape)

    for k in range(0, BASES, 2):
        first, second = table[k], table[k + 1]
        p, q, r, s = entry(first, k), entry(second, k), entry(first, k + 1), entry(second, k + 1)
        inverse = 1.0 / (p * s - q * r)
        for c in range(k + 2, BASES + 1):
            above, below = entry(table[c], k), entry(table[c], k + 1)
            x = (s * above - q * below) * inverse
            y = (p * below - r * above) * inverse
            rest = table[c] - (first * x + second * y)
            table[c] = jnp.where(lanes == k * TILE, x, jnp.where(lanes == (k + 1) * TILE, y, rest))
    exact = [entry(table[BASES], a) for a in range(BASES)]
    high = [value.astype(jnp.bfloat16).astype(jnp.float32) for value in exact]
    terms = high + [value - upper for value, upper in zip(exact, high)]
    group = lanes // TILE
    spread = []
    for first in range(0, len(terms), LANES // TILE):
        several = terms[first : first + LANES // TILE]
        line = several[0]
        for g in range(1, len(several)):
            line = jnp.where(group >= g, several[g], line)
        spread.append(line)
    width = len(terms) * TILE
    spread = jnp.concatenate(spread, axis=1)[:, :width]
    line = lax.broadcasted_iota(jnp.int32, (TILE, width), 0)
    lane = lax.broadcasted_iota(jnp.int32, (TILE, width), 1)
    same = line == lane % TILE
    order_copy.wait()
    copies = []
    for slot in range(slots):
        blocks = [
            jnp.where(same, spread[slot * cap + k : slot * cap + k + 1, :], 0.0).astype(jnp.bfloat16)
            for k in range(cap)
        ]
        basis = basis_ref[slot]
        fitted = jnp.dot(
            jnp.concatenate(blocks, axis=0),
            jnp.concatenate([basis, basis], axis=0),
            preferred_element_type=jnp.float32,
        )
        for k in range(cap):
            j = order_ref[slot * cap + k]
            place = slot * cap + k
            for g in range(tiles):
                part = fitted[k * TILE : (k + 1) * TILE, g * cols : (g + 1) * cols]
                image = image_ref[j, g * TILE : (g + 1) * TILE, :].astype(jnp.float32)
                difference_ref[place, g * TILE : (g + 1) * TILE, :] = (image - part).astype(jnp.bfloat16)
            copy = pltpu.make_async_copy(difference_ref.at[place], difference_hbm.at[j], sem.at[place])
            copy.start()
            copies.append(copy)
    for copy in copies:
        copy.wait()


def call(kernel, name, outs, in_specs, out_specs, args, scratch=(), flops=0, size=0, limit=VMEM_LIMIT):
    return pl.pallas_call(
        kernel,
        out_shape=outs,
        in_specs=in_specs,
        out_specs=out_specs,
        scratch_shapes=list(scratch),
        name=name,
        compiler_params=pltpu.CompilerParams(vmem_limit_bytes=limit),
        cost_estimate=pl.CostEstimate(flops=flops, bytes_accessed=size, transcendentals=0),
    )(*args)


def body(images, mask_bits, visit_weight, intersection, patch_owner):
    visits = lax.axis_size("visit")
    strips = lax.axis_size("strip")
    _, pieces, rows, cols = images.shape
    slots = visits // 2
    cap = pieces // slots
    tiles = rows // TILE
    shape = jax.ShapeDtypeStruct
    bf16, f32 = jnp.bfloat16, jnp.float32
    image = images[0]
    mask = mask_bits[0]
    halves = strips == 2 and visits == 4
    half = rows // 2 if halves else rows
    ids = intersection[:, 0]
    label_rows = -(-slots // TILE) * TILE
    message_rows = slots * 2 * half * (cols // LANES)
    message_shape = (label_rows + message_rows, LANES)

    message = call(
        functools.partial(first_kernel, slots, cap, half, halves),
        "first_sums",
        shape(message_shape, bf16),
        [HBM] * 4,
        HBM,
        (ids, visit_weight, image, mask),
        scratch=[
            pltpu.VMEM(message_shape, bf16),
            pltpu.SMEM((pieces,), jnp.int32),
            pltpu.SMEM((pieces,), f32),
            pltpu.SMEM((pieces,), jnp.int32),
            pltpu.VMEM((1, pieces), bf16),
            pltpu.VMEM((pieces, half, cols), bf16),
            pltpu.VMEM((pieces, half, cols), jnp.int32),
            pltpu.SemaphoreType.DMA((2,)),
            pltpu.SemaphoreType.DMA((half // TILE, 2)),
            pltpu.SemaphoreType.DMA((half // TILE,)),
        ],
        size=2 << 20,
        limit=FETCH_LIMIT,
    )

    sorted_shape = shape((slots, cap * TILE, tiles * cols), bf16)
    sorted_outs = (sorted_shape, sorted_shape, shape((pieces,), jnp.int32))
    if halves:

        shifts = sorted(range(1, visits), key=lambda shift: min(shift, visits - shift))

        def everyone(value):
            others = [
                lax.ppermute(value, "visit", [(i, i ^ shift) for i in range(visits)]) for shift in shifts
            ]
            return [value] + others

        firsts = everyone(message)
        second = call(
            functools.partial(second_kernel, slots, cap, half),
            "second_sums",
            shape((message_rows, LANES), bf16),
            [SMEM] + [VMEM] * 3,
            VMEM,
            (ids, visit_weight, image, mask),
            scratch=[pltpu.SMEM((pieces,), jnp.int32), pltpu.SMEM((pieces,), f32)],
            size=1 << 20,
        )
        seconds = everyone(second)
    usable, masked, order = call(
        functools.partial(sort_kernel, slots, cap),
        "sorted_usable",
        sorted_outs,
        [SMEM, VMEM, VMEM],
        (VMEM, VMEM, SMEM),
        (ids, image, mask),
        size=3 << 20,
    )
    normal_outs = (shape((slots, BASES * TILE, tiles * cols), bf16), shape((pieces, 128), f32))
    normal_scratch = [
        pltpu.VMEM((3, slots, rows, cols), bf16),
        pltpu.VMEM(((BASES + 1) * cap * TILE, tiles * cols), bf16),
    ]
    across = jnp.asarray(across_matrices(cols))
    if halves:
        template, edge = call(
            functools.partial(border_kernel, slots, half),
            "border",
            (shape((slots, half, cols), bf16), shape((slots, TILE, cols), bf16)),
            [VMEM] * visits,
            (VMEM,) * 2,
            firsts,
            size=1 << 20,
        )
        halo = lax.ppermute(edge, "strip", [(0, 1), (1, 0)])
        low, high = list(range(half)), list(range(half, rows))
        vertical = np.stack(
            [
                vertical_matrix(rows, high + low + list(range(rows, rows + TILE))),
                vertical_matrix(rows, low + high + list(range(-TILE, 0))),
            ]
        )
        basis, sums = call(
            functools.partial(halves_kernel, slots, cap, visits, half),
            "normal_equations",
            normal_outs,
            [VMEM] * (2 * visits + 6),
            (VMEM,) * 2,
            (*firsts, *seconds, template, halo, jnp.asarray(vertical), across, usable, masked),
            scratch=[pltpu.VMEM((slots, half, cols), bf16)] + normal_scratch,
            size=2 << 20,
        )
        coadd = call(
            functools.partial(own_kernel, slots, visits, half),
            "own_patch",
            shape((rows, cols), bf16),
            [SMEM, ANY] + [VMEM] * (2 * visits),
            VMEM,
            (patch_owner, sums, *firsts, *seconds),
            size=1 << 20,
        )
        totals = [sums, lax.ppermute(sums, "strip", [(0, 1), (1, 0)])]
    else:
        template, coadd, edge = call(
            functools.partial(gathered_kernel, slots),
            "combine",
            (shape((slots, rows, cols), bf16), shape((rows, cols), bf16), shape((slots, 2 * TILE, cols), bf16)),
            [SMEM, VMEM],
            (VMEM,) * 3,
            (patch_owner, lax.all_gather(message, "visit")),
            scratch=[pltpu.VMEM((slots + 1, 2, rows, cols), f32)],
            size=1 << 20,
        )
        below = lax.ppermute(edge[:, TILE:], "strip", [(i, i + 1) for i in range(strips - 1)])
        above = lax.ppermute(edge[:, :TILE], "strip", [(i + 1, i) for i in range(strips - 1)])
        around = list(range(rows)) + list(range(-TILE, 0)) + list(range(rows, rows + TILE))
        basis, sums = call(
            functools.partial(normal_kernel, slots, cap),
            "normal_equations",
            normal_outs,
            [VMEM] * 7,
            (VMEM, VMEM),
            (template, below, above, jnp.asarray(vertical_matrix(rows, around)[None]), across, usable, masked),
            scratch=normal_scratch,
            size=2 << 20,
        )
        totals = [lax.psum(sums, "strip")]
    difference = call(
        functools.partial(fit_kernel, slots, cap),
        "fit",
        shape((pieces, rows, cols), bf16),
        [ANY] + [VMEM] * (len(totals) + 2),
        HBM,
        (order, *totals, basis, image),
        scratch=[
            pltpu.VMEM((pieces, rows, cols), bf16),
            pltpu.SMEM((pieces,), jnp.int32),
            pltpu.SemaphoreType.DMA((1,)),
            pltpu.SemaphoreType.DMA((pieces,)),
        ],
        size=2 << 20,
    )
    return (coadd[None, None], difference[None])


def solution(mesh):
    in_specs = (
        P("band", ("groups", "visit"), "strip", None),
        P("band", ("groups", "visit"), "strip", None),
        P("band", ("groups", "visit")),
        P(("groups", "visit"), None),
        P("groups"),
    )
    out_specs = (
        P("band", ("groups", "visit"), "strip", None),
        P("band", ("groups", "visit"), "strip", None),
    )
    return jax.shard_map(body, mesh=mesh, in_specs=in_specs, out_specs=out_specs, check_vma=False)
```

```python
import functools

import jax
import jax.numpy as jnp
import ml_dtypes
import numpy as np
from jax import lax
from jax.experimental import pallas as pl
from jax.experimental.pallas import tpu as pltpu
from jax.sharding import PartitionSpec as P

BASES = 6
HALF = 9
TILE = 16
LANES = 128
basis_rows = (0, 0, 1, 0, 2, 1)
basis_cols = (0, 1, 0, 2, 0, 1)
VMEM_LIMIT = 48 * 1024 * 1024
FETCH_LIMIT = 56 * 1024 * 1024

VMEM = pl.BlockSpec(memory_space=pltpu.VMEM)
SMEM = pl.BlockSpec(memory_space=pltpu.SMEM)
HBM = pl.BlockSpec(memory_space=pltpu.HBM)
ANY = pl.BlockSpec(memory_space=pl.ANY)


def tap_rows():
    offsets = np.arange(2 * HALF + 1).astype(np.float64) - HALF
    gaussian = np.exp(-offsets * offsets / 18.0)
    squared = gaussian * gaussian
    centre = np.sum(offsets * offsets * squared) / np.sum(squared)
    table = np.stack([gaussian, offsets * gaussian, (offsets * offsets - centre) * gaussian])
    table = table / np.sqrt(np.sum(table * table, axis=1, keepdims=True))
    return table.astype(ml_dtypes.bfloat16)


def across_matrices(cols):
    taps = tap_rows()
    distance = np.arange(cols)[:, None] - np.arange(cols)[None, :] + HALF
    inside = (distance >= 0) & (distance <= 2 * HALF)
    return np.where(inside[None], taps[:, np.clip(distance, 0, 2 * HALF)], 0).astype(ml_dtypes.bfloat16)


def vertical_matrix(rows, sources):
    taps = tap_rows()
    distance = np.asarray(sources)[None, :] - np.arange(rows)[:, None] + HALF
    inside = (distance >= 0) & (distance <= 2 * HALF)
    table = np.where(inside[None], taps[:, np.clip(distance, 0, 2 * HALF)], 0)
    return table.reshape(3 * rows, len(sources)).astype(ml_dtypes.bfloat16)


def unusable(mask):
    return jnp.bitwise_and(mask, 3) == 3


def piece_order(ids_ref, order_ref):
    pieces = order_ref.shape[0]
    ids = [ids_ref[j] for j in range(pieces)]
    for j in range(pieces):
        place = jnp.int32(0)
        for i in range(pieces):
            if i < j:
                place = place + (ids[i] <= ids[j]).astype(jnp.int32)
            elif i > j:
                place = place + (ids[i] < ids[j]).astype(jnp.int32)
        order_ref[place] = j


def piece_weights(weight_ref, splat_ref):
    weights = weight_ref[...].astype(jnp.float32)
    for j in range(splat_ref.shape[0]):
        splat_ref[j] = weights[0, j]


def windows(half, halves):
    if not halves:
        return 0, 0
    strip = lax.axis_index("strip")
    return pl.multiple_of((1 - strip) * half, TILE), pl.multiple_of(strip * half, TILE)


def put_sums(slots, cap, order_ref, weight_ref, image_of, mask_of, message_ref, base):
    cols = image_of(0).shape[1]
    parts = cols // LANES
    for slot in range(slots):
        numerator = jnp.zeros((TILE, cols), jnp.float32)
        denominator = jnp.zeros((TILE, cols), jnp.float32)
        for k in range(cap):
            j = order_ref[slot * cap + k]
            weight = jnp.where(unusable(mask_of(j)), 0.0, weight_ref[j])
            denominator = denominator + weight
            numerator = numerator + weight * image_of(j).astype(jnp.float32)
        for kind, value in enumerate((numerator.astype(jnp.bfloat16), denominator.astype(jnp.bfloat16))):
            for part in range(parts):
                at = base + ((slot * 2 + kind) * parts + part) * TILE
                message_ref[at : at + TILE, :] = value[:, part * LANES : (part + 1) * LANES]


def first_kernel(slots, cap, half, halves, ids_hbm, weight_hbm, image_hbm, mask_hbm, message_hbm, *refs):
    message_ref, order_ref, splat_ref, ids_ref, weight_ref, image_ref, mask_ref, small_sem, sem, out_sem = refs
    tiles = half // TILE
    step = slots * 2 * TILE * (image_ref.shape[2] // LANES)
    first = windows(half, halves)[0]
    small = [
        pltpu.make_async_copy(ids_hbm, ids_ref, small_sem.at[0]),
        pltpu.make_async_copy(weight_hbm, weight_ref, small_sem.at[1]),
    ]
    large = []
    for g in range(tiles):
        source = pl.ds(first + g * TILE, TILE)
        here = slice(g * TILE, (g + 1) * TILE)
        large.append(
            (
                pltpu.make_async_copy(mask_hbm.at[:, source, :], mask_ref.at[:, here, :], sem.at[g, 0]),
                pltpu.make_async_copy(image_hbm.at[:, source, :], image_ref.at[:, here, :], sem.at[g, 1]),
            )
        )
    for copy in small:
        copy.start()
    for pair in large:
        for copy in pair:
            copy.start()
    for copy in small:
        copy.wait()
    piece_order(ids_ref, order_ref)
    piece_weights(weight_ref, splat_ref)
    label_rows = message_ref.shape[0] - tiles * step
    line = lax.broadcasted_iota(jnp.int32, (label_rows, LANES), 0)
    labels = jnp.zeros((label_rows, LANES), jnp.float32)
    for slot in range(slots):
        labels = jnp.where(line == slot, ids_ref[order_ref[slot * cap]].astype(jnp.float32), labels)
    message_ref[:label_rows, :] = labels.astype(jnp.bfloat16)
    done, copies = 0, []
    for g in range(tiles):
        for copy in large[g]:
            copy.wait()
        here = slice(g * TILE, (g + 1) * TILE)
        base = label_rows + g * step
        put_sums(
            slots,
            cap,
            order_ref,
            splat_ref,
            lambda j, here=here: image_ref[j, here, :],
            lambda j, here=here: mask_ref[j, here, :],
            message_ref,
            base,
        )
        ready = pl.ds(done, base + step - done)
        copies.append(pltpu.make_async_copy(message_ref.at[ready, :], message_hbm.at[ready, :], out_sem.at[g]))
        copies[-1].start()
        done = base + step
    for copy in copies:
        copy.wait()


def second_kernel(slots, cap, half, ids_ref, weight_ref, image_ref, mask_ref, *refs):
    message_ref, order_ref, splat_ref = refs
    first = windows(half, True)[1]
    step = slots * 2 * TILE * (image_ref.shape[2] // LANES)
    piece_order(ids_ref, order_ref)
    piece_weights(weight_ref, splat_ref)
    for g in range(half // TILE):
        here = pl.ds(first + g * TILE, TILE)
        put_sums(
            slots,
            cap,
            order_ref,
            splat_ref,
            lambda j, here=here: image_ref[j, here, :],
            lambda j, here=here: mask_ref[j, here, :],
            message_ref,
            g * step,
        )


def sort_kernel(slots, cap, ids_ref, image_ref, mask_ref, usable_ref, masked_ref, order_ref):
    piece_order(ids_ref, order_ref)
    put_sorted(slots, cap, order_ref, image_ref, mask_ref, usable_ref, masked_ref)


def put_sorted(slots, cap, order_ref, image_ref, mask_ref, usable_ref, masked_ref):
    rows, cols = image_ref.shape[1:]
    for slot in range(slots):
        for k in range(cap):
            j = order_ref[slot * cap + k]
            for g in range(rows // TILE):
                lines = slice(g * TILE, (g + 1) * TILE)
                usable = jnp.where(unusable(mask_ref[j, lines, :]), 0.0, 1.0).astype(jnp.bfloat16)
                at = (slot, slice(k * TILE, (k + 1) * TILE), slice(g * cols, (g + 1) * cols))
                usable_ref[at] = usable
                masked_ref[at] = usable * image_ref[j, lines, :]


def owned_patch(owner_ref):
    visit = lax.axis_index("visit")
    mine = jnp.int32(0)
    for p in range(owner_ref.shape[0]):
        mine = jnp.where(owner_ref[p] == visit, p, mine)
    return mine.astype(jnp.float32)


def picks(labels, own_labels, mine, slots, slot):
    label = labels[slot : slot + 1, :]
    hits = [label == own_labels[t : t + 1, :] for t in range(slots)]
    if mine is not None:
        hits.append(label == mine)
    return [hit.astype(jnp.float32) for hit in hits]


def quotient(numerator, denominator):
    return (numerator / jnp.maximum(denominator, 1.0)).astype(jnp.bfloat16)


def combine(slots, rows, cols, base, mine, labels, sources, put):
    parts = cols // LANES
    labels = [value.astype(jnp.float32) for value in labels]
    hits = [[picks(label, labels[0], mine, slots, slot) for slot in range(slots)] for label in labels]
    targets = range(slots) if mine is None else range(slots, slots + 1)
    for first in range(0, rows, TILE):
        for part in range(parts):
            sums = [[jnp.zeros((TILE, LANES), jnp.float32) for _ in range(2)] for _ in range(slots + 1)]
            for d, ref in enumerate(sources):
                for slot in range(slots):
                    for kind in range(2):
                        at = base + (first * slots * 2 + (slot * 2 + kind) * TILE) * parts + part * TILE
                        value = ref[at : at + TILE, :].astype(jnp.float32)
                        for t in targets:
                            if d == 0 and t < slots:
                                if t == slot:
                                    sums[t][kind] = sums[t][kind] + value
                            else:
                                sums[t][kind] = sums[t][kind] + hits[d][slot][t] * value
            lanes = slice(part * LANES, (part + 1) * LANES)
            for t in targets:
                put(t, first, lanes, quotient(*sums[t]))


def message_base(ref, slots, rows, cols):
    return ref.shape[0] - slots * 2 * rows * (cols // LANES)


def border_kernel(slots, rows, *refs):
    sources, (template_ref, edge_ref) = refs[:-2], refs[-2:]
    cols = template_ref.shape[2]
    base = message_base(sources[0], slots, rows, cols)

    def put(t, first, lanes, value):
        template_ref[t, first : first + TILE, lanes] = value

    combine(slots, rows, cols, base, None, [ref[:base, :] for ref in sources], sources, put)
    at = pl.multiple_of((1 - lax.axis_index("strip")) * (rows - TILE), TILE)
    edge_ref[...] = template_ref[:, pl.ds(at, TILE), :]


def own_kernel(slots, count, rows, owner_ref, after_ref, *refs):
    firsts, seconds, coadd_ref = refs[:count], refs[count : 2 * count], refs[2 * count]
    del after_ref
    cols = coadd_ref.shape[1]
    base = message_base(firsts[0], slots, rows, cols)
    labels = [ref[:base, :] for ref in firsts]
    mine = owned_patch(owner_ref)
    for sources, skip, start in zip((firsts, seconds), (base, 0), windows(rows, True)):

        def put(t, first, lanes, value, start=start):
            coadd_ref[pl.ds(start + first, TILE), lanes] = value

        combine(slots, rows, cols, skip, mine, labels, sources, put)


def gathered_kernel(slots, owner_ref, stacked_ref, template_ref, coadd_ref, edge_ref, total_ref):
    rows, cols = coadd_ref.shape
    parts = cols // LANES
    base = stacked_ref.shape[1] - rows * slots * 2 * parts
    mine = owned_patch(owner_ref)
    own_labels = stacked_ref[lax.axis_index("visit"), :base, :].astype(jnp.float32)
    total_ref[...] = jnp.zeros_like(total_ref)

    def add_source(d, carry):
        labels = stacked_ref[d, :base, :].astype(jnp.float32)
        for slot in range(slots):
            pick = picks(labels, own_labels, mine, slots, slot)
            for kind in range(2):
                for first in range(0, rows, TILE):
                    for part in range(parts):
                        at = base + (first * slots * 2 + (slot * 2 + kind) * TILE) * parts + part * TILE
                        value = stacked_ref[d, at : at + TILE, :].astype(jnp.float32)
                        lanes = slice(part * LANES, (part + 1) * LANES)
                        for t in range(slots + 1):
                            total_ref[t, kind, first : first + TILE, lanes] += pick[t] * value
        return carry

    lax.fori_loop(0, stacked_ref.shape[0], add_source, 0)
    for t in range(slots):
        template_ref[t] = quotient(total_ref[t, 0], total_ref[t, 1])
    coadd_ref[...] = quotient(total_ref[slots, 0], total_ref[slots, 1])
    edge_ref[:, :TILE, :] = template_ref[:, :TILE, :]
    edge_ref[:, TILE:, :] = template_ref[:, rows - TILE :, :]


def halves_kernel(slots, cap, count, rows, *refs):
    firsts, seconds, refs = refs[:count], refs[count : 2 * count], refs[2 * count :]
    template_ref, halo_ref, vertical_ref, across_ref, usable_ref, masked_ref = refs[:6]
    basis_ref, sums_ref, second_ref, smooth_ref, left_ref = refs[6:]
    cols = template_ref.shape[2]
    base = message_base(firsts[0], slots, rows, cols)

    def put(t, first, lanes, value):
        second_ref[t, first : first + TILE, lanes] = value

    combine(slots, rows, cols, 0, None, [ref[:base, :] for ref in firsts], seconds, put)
    normal_equations(
        slots,
        cap,
        [template_ref, second_ref, halo_ref],
        vertical_ref[lax.axis_index("strip")],
        across_ref,
        usable_ref,
        masked_ref,
        basis_ref,
        sums_ref,
        smooth_ref,
        left_ref,
    )


def normal_kernel(slots, cap, template_ref, below_ref, above_ref, vertical_ref, *refs):
    normal_equations(slots, cap, [template_ref, below_ref, above_ref], vertical_ref[0], *refs)


def normal_equations(
    slots, cap, parts, vertical, across_ref, usable_ref, masked_ref, basis_ref, sums_ref, smooth_ref, left_ref
):
    rows, cols = smooth_ref.shape[2:]
    tiles = rows // TILE
    for slot in range(slots):
        extended = jnp.concatenate([ref[slot] for ref in parts], axis=0)
        smooth = jnp.dot(vertical, extended, preferred_element_type=jnp.float32)
        for k in range(3):
            smooth_ref[k, slot] = smooth[k * rows : (k + 1) * rows].astype(jnp.bfloat16)
    for c in range(3):
        users = [a for a in range(BASES) if basis_cols[a] == c]
        for slot in range(slots):
            stacked = jnp.concatenate([smooth_ref[basis_rows[a], slot] for a in users], axis=0)
            planes = jnp.dot(stacked, across_ref[c], preferred_element_type=jnp.float32).astype(jnp.bfloat16)
            for n, a in enumerate(users):
                for g in range(tiles):
                    at = n * rows + g * TILE
                    basis_ref[slot, a * TILE : (a + 1) * TILE, g * cols : (g + 1) * cols] = planes[at : at + TILE]
    group = cap * TILE
    height = BASES * group + group
    for slot in range(slots):
        for a in range(BASES):
            plane = basis_ref[slot, a * TILE : (a + 1) * TILE, :]
            for k in range(cap):
                at = a * group + k * TILE
                left_ref[at : at + TILE, :] = plane * usable_ref[slot, k * TILE : (k + 1) * TILE, :]
        left_ref[BASES * group :, :] = masked_ref[slot]
        product = lax.dot_general(
            left_ref[...], basis_ref[slot], (((1,), (1,)), ((), ())), preferred_element_type=jnp.float32
        )
        width = product.shape[1]
        line = lax.broadcasted_iota(jnp.int32, (TILE, width), 0)
        lane = lax.broadcasted_iota(jnp.int32, (TILE, width), 1)
        same = line == lane % TILE
        product = jnp.where(same[None], product.reshape(height // TILE, TILE, width), 0.0)
        product = jnp.sum(product, axis=1)
        product = jnp.concatenate([product, jnp.zeros((height // TILE, 128 - width), jnp.float32)], axis=1)
        for step in (1, 2, 4, 8):
            product = product + pltpu.roll(product, 128 - step, 1)
        lanes = lax.broadcasted_iota(jnp.int32, product.shape, 1)
        product = jnp.where(lanes % TILE == 0, product, 0.0)
        packed = product[:cap]
        for a in range(1, BASES + 1):
            packed = packed + pltpu.roll(product[a * cap : (a + 1) * cap], a, 1)
        sums_ref[slot * cap : (slot + 1) * cap, :] = packed


def fit_kernel(slots, cap, order_any, *refs):
    sums_refs, refs = refs[:-7], refs[-7:]
    basis_ref, image_ref, difference_hbm, difference_ref, order_ref, order_sem, sem = refs
    order_copy = pltpu.make_async_copy(order_any, order_ref, order_sem.at[0])
    order_copy.start()
    rows, cols = image_ref.shape[1:]
    tiles = rows // TILE
    total = sums_refs[0][...]
    for ref in sums_refs[1:]:
        total = total + ref[...]
    pieces = total.shape[0]
    lanes = lax.broadcasted_iota(jnp.int32, (pieces, 128), 1)
    table = []
    for c in range(BASES + 1):
        line = total if c == 0 else pltpu.roll(total, 128 - c, 1)
        if c < BASES:
            line = line + jnp.where(lanes == c * TILE, 1.0, 0.0)
        table.append(line)
    def entry(line, a):
        return jnp.broadcast_to(line[:, a * TILE : a * TILE + 1], line.shape)

    for k in range(0, BASES, 2):
        first, second = table[k], table[k + 1]
        p, q, r, s = entry(first, k), entry(second, k), entry(first, k + 1), entry(second, k + 1)
        inverse = 1.0 / (p * s - q * r)
        for c in range(k + 2, BASES + 1):
            above, below = entry(table[c], k), entry(table[c], k + 1)
            x = (s * above - q * below) * inverse
            y = (p * below - r * above) * inverse
            rest = table[c] - (first * x + second * y)
            table[c] = jnp.where(lanes == k * TILE, x, jnp.where(lanes == (k + 1) * TILE, y, rest))
    exact = [entry(table[BASES], a) for a in range(BASES)]
    high = [value.astype(jnp.bfloat16).astype(jnp.float32) for value in exact]
    terms = high + [value - upper for value, upper in zip(exact, high)]
    group = lanes // TILE
    spread = []
    for first in range(0, len(terms), LANES // TILE):
        several = terms[first : first + LANES // TILE]
        line = several[0]
        for g in range(1, len(several)):
            line = jnp.where(group >= g, several[g], line)
        spread.append(line)
    width = len(terms) * TILE
    spread = jnp.concatenate(spread, axis=1)[:, :width]
    line = lax.broadcasted_iota(jnp.int32, (TILE, width), 0)
    lane = lax.broadcasted_iota(jnp.int32, (TILE, width), 1)
    same = line == lane % TILE
    order_copy.wait()
    copies = []
    for slot in range(slots):
        blocks = [
            jnp.where(same, spread[slot * cap + k : slot * cap + k + 1, :], 0.0).astype(jnp.bfloat16)
            for k in range(cap)
        ]
        basis = basis_ref[slot]
        fitted = jnp.dot(
            jnp.concatenate(blocks, axis=0),
            jnp.concatenate([basis, basis], axis=0),
            preferred_element_type=jnp.float32,
        )
        for k in range(cap):
            j = order_ref[slot * cap + k]
            place = slot * cap + k
            for g in range(tiles):
                part = fitted[k * TILE : (k + 1) * TILE, g * cols : (g + 1) * cols]
                image = image_ref[j, g * TILE : (g + 1) * TILE, :].astype(jnp.float32)
                difference_ref[place, g * TILE : (g + 1) * TILE, :] = (image - part).astype(jnp.bfloat16)
            copy = pltpu.make_async_copy(difference_ref.at[place], difference_hbm.at[j], sem.at[place])
            copy.start()
            copies.append(copy)
    for copy in copies:
        copy.wait()


def call(kernel, name, outs, in_specs, out_specs, args, scratch=(), flops=0, size=0, limit=VMEM_LIMIT):
    return pl.pallas_call(
        kernel,
        out_shape=outs,
        in_specs=in_specs,
        out_specs=out_specs,
        scratch_shapes=list(scratch),
        name=name,
        compiler_params=pltpu.CompilerParams(vmem_limit_bytes=limit),
        cost_estimate=pl.CostEstimate(flops=flops, bytes_accessed=size, transcendentals=0),
    )(*args)


def body(images, mask_bits, visit_weight, intersection, patch_owner):
    visits = lax.axis_size("visit")
    strips = lax.axis_size("strip")
    _, pieces, rows, cols = images.shape
    slots = visits // 2
    cap = pieces // slots
    tiles = rows // TILE
    shape = jax.ShapeDtypeStruct
    bf16, f32 = jnp.bfloat16, jnp.float32
    image = images[0]
    mask = mask_bits[0]
    halves = strips == 2 and visits == 4
    half = rows // 2 if halves else rows
    ids = intersection[:, 0]
    label_rows = -(-slots // TILE) * TILE
    message_rows = slots * 2 * half * (cols // LANES)
    message_shape = (label_rows + message_rows, LANES)

    message = call(
        functools.partial(first_kernel, slots, cap, half, halves),
        "first_sums",
        shape(message_shape, bf16),
        [HBM] * 4,
        HBM,
        (ids, visit_weight, image, mask),
        scratch=[
            pltpu.VMEM(message_shape, bf16),
            pltpu.SMEM((pieces,), jnp.int32),
            pltpu.SMEM((pieces,), f32),
            pltpu.SMEM((pieces,), jnp.int32),
            pltpu.VMEM((1, pieces), bf16),
            pltpu.VMEM((pieces, half, cols), bf16),
            pltpu.VMEM((pieces, half, cols), jnp.int32),
            pltpu.SemaphoreType.DMA((2,)),
            pltpu.SemaphoreType.DMA((half // TILE, 2)),
            pltpu.SemaphoreType.DMA((half // TILE,)),
        ],
        size=2 << 20,
        limit=FETCH_LIMIT,
    )

    sorted_shape = shape((slots, cap * TILE, tiles * cols), bf16)
    sorted_outs = (sorted_shape, sorted_shape, shape((pieces,), jnp.int32))
    if halves:

        shifts = sorted(range(1, visits), key=lambda shift: min(shift, visits - shift))

        def everyone(value):
            others = [
                lax.ppermute(value, "visit", [(i, i ^ shift) for i in range(visits)]) for shift in shifts
            ]
            return [value] + others

        firsts = everyone(message)
        second = call(
            functools.partial(second_kernel, slots, cap, half),
            "second_sums",
            shape((message_rows, LANES), bf16),
            [SMEM] + [VMEM] * 3,
            VMEM,
            (ids, visit_weight, image, mask),
            scratch=[pltpu.SMEM((pieces,), jnp.int32), pltpu.SMEM((pieces,), f32)],
            size=1 << 20,
        )
        seconds = everyone(second)
    usable, masked, order = call(
        functools.partial(sort_kernel, slots, cap),
        "sorted_usable",
        sorted_outs,
        [SMEM, VMEM, VMEM],
        (VMEM, VMEM, SMEM),
        (ids, image, mask),
        size=3 << 20,
    )
    normal_outs = (shape((slots, BASES * TILE, tiles * cols), bf16), shape((pieces, 128), f32))
    normal_scratch = [
        pltpu.VMEM((3, slots, rows, cols), bf16),
        pltpu.VMEM(((BASES + 1) * cap * TILE, tiles * cols), bf16),
    ]
    across = jnp.asarray(across_matrices(cols))
    if halves:
        template, edge = call(
            functools.partial(border_kernel, slots, half),
            "border",
            (shape((slots, half, cols), bf16), shape((slots, TILE, cols), bf16)),
            [VMEM] * visits,
            (VMEM,) * 2,
            firsts,
            size=1 << 20,
        )
        halo = lax.ppermute(edge, "strip", [(0, 1), (1, 0)])
        low, high = list(range(half)), list(range(half, rows))
        vertical = np.stack(
            [
                vertical_matrix(rows, high + low + list(range(rows, rows + TILE))),
                vertical_matrix(rows, low + high + list(range(-TILE, 0))),
            ]
        )
        basis, sums = call(
            functools.partial(halves_kernel, slots, cap, visits, half),
            "normal_equations",
            normal_outs,
            [VMEM] * (2 * visits + 6),
            (VMEM,) * 2,
            (*firsts, *seconds, template, halo, jnp.asarray(vertical), across, usable, masked),
            scratch=[pltpu.VMEM((slots, half, cols), bf16)] + normal_scratch,
            size=2 << 20,
        )
        coadd = call(
            functools.partial(own_kernel, slots, visits, half),
            "own_patch",
            shape((rows, cols), bf16),
            [SMEM, ANY] + [VMEM] * (2 * visits),
            VMEM,
            (patch_owner, sums, *firsts, *seconds),
            size=1 << 20,
        )
        totals = [sums, lax.ppermute(sums, "strip", [(0, 1), (1, 0)])]
    else:
        template, coadd, edge = call(
            functools.partial(gathered_kernel, slots),
            "combine",
            (shape((slots, rows, cols), bf16), shape((rows, cols), bf16), shape((slots, 2 * TILE, cols), bf16)),
            [SMEM, VMEM],
            (VMEM,) * 3,
            (patch_owner, lax.all_gather(message, "visit")),
            scratch=[pltpu.VMEM((slots + 1, 2, rows, cols), f32)],
            size=1 << 20,
        )
        below = lax.ppermute(edge[:, TILE:], "strip", [(i, i + 1) for i in range(strips - 1)])
        above = lax.ppermute(edge[:, :TILE], "strip", [(i + 1, i) for i in range(strips - 1)])
        around = list(range(rows)) + list(range(-TILE, 0)) + list(range(rows, rows + TILE))
        basis, sums = call(
            functools.partial(normal_kernel, slots, cap),
            "normal_equations",
            normal_outs,
            [VMEM] * 7,
            (VMEM, VMEM),
            (template, below, above, jnp.asarray(vertical_matrix(rows, around)[None]), across, usable, masked),
            scratch=normal_scratch,
            size=2 << 20,
        )
        totals = [lax.psum(sums, "strip")]
    difference = call(
        functools.partial(fit_kernel, slots, cap),
        "fit",
        shape((pieces, rows, cols), bf16),
        [ANY] + [VMEM] * (len(totals) + 2),
        HBM,
        (order, *totals, basis, image),
        scratch=[
            pltpu.VMEM((pieces, rows, cols), bf16),
            pltpu.SMEM((pieces,), jnp.int32),
            pltpu.SemaphoreType.DMA((1,)),
            pltpu.SemaphoreType.DMA((pieces,)),
        ],
        size=2 << 20,
    )
    return (coadd[None, None], difference[None])


def solution(mesh):
    in_specs = (
        P("band", ("groups", "visit"), "strip", None),
        P("band", ("groups", "visit"), "strip", None),
        P("band", ("groups", "visit")),
        P(("groups", "visit"), None),
        P("groups"),
    )
    out_specs = (
        P("band", ("groups", "visit"), "strip", None),
        P("band", ("groups", "visit"), "strip", None),
    )
    return jax.shard_map(body, mesh=mesh, in_specs=in_specs, out_specs=out_specs, check_vma=False)
```
